256 devices in a mesh: ctx: 8 (over z), chan: 8 (over y, core), req: 4 (over x).
Axes of the slice: x: 4, y: 4, z: 8, core: 2. Of those that a mesh axis runs over, the one named last changes fastest.
Arguments:
- window_input: bfloat16 [4096, 8192], P(('req', 'ctx'), 'chan'), parts along dimension 0, may hold values from -6 to 6
- gate_values: bfloat16 [4096, 8192], P(('req', 'ctx'), 'chan'), parts along dimension 0, may hold values from -6 to 6
- page_pool: bfloat16 [4096, 8, 8192], P(('req', 'ctx', 'chan')), parts along dimension 0, may hold values from -6 to 6
- page_table: int32 [2048], P('req'), parts along dimension 0, may hold values from 0 to 1023, as said below
- filter_len: int32 [8192], P('chan'), may hold values from 1024 to 4096
- residues: float32 [8192, 16], P('chan'), may hold values from -0.06 to 0.06
- decays: float32 [8192, 16], P('chan'), may hold values from 0.0001 to 0.1
- skip_gain: float32 [8192], P('chan'), may hold values from 0.5 to 1.5
Outputs:
- gated_output: bfloat16 [4096, 8192], P(('req', 'ctx'), 'chan'), parts along dimension 0
The draws below stay inside these ranges and needn't reach their ends.
There are 4 independent parts, one for each index of `req`. The reference program is written for one: setup_inputs(seed, part) draws one part's arguments, and reference() takes and returns one part's arrays. A program takes and returns all parts, laid end to end along the dimension named above; an argument that names none is the same for every part. Nothing has to cross between parts.
Inputs may be any that keep to these rules, and one draw needn't show every extreme that they name: `page_table`: the entries are distinct; pool page i lies on device i // 16 of ctx+chan. Of the 64 cache pages of each aligned block of the table (the cached positions of one index of ctx), at most 2 lie on one device, and in every block some device holds exactly 2.
All inputs are finite; a program needn't handle non-finite values.
Results may differ from the reference program's by a relative error of at most 0.009.
Values may be sent and summed in bfloat16 or wider, within the bound.
No kernel may reach another device: no remote copies, remote signals or barrier semaphores. Data moves between devices by JAX's collectives and lax.ppermute only.
A program may use at most 64 MiB of HBM per device.

```python
import math
import jax
import jax.numpy as jnp
from jax import lax

D = 8192
MODES = 16
PAGE = 8
CACHE = 4096
WIN = 1024
SEQ = 5120
PPD = 64
CAP = 2
POOL_DEV = 16
POOL = 1024
N_CTX = 8
N_CHAN = 8


def draw_page_table(key, part):
    owner_count = N_CTX * N_CHAN

    def block_owners(block_key):
        key_fullest, key_rest, key_order = jax.random.split(block_key, 3)
        fullest = jax.random.randint(key_fullest, (), 0, owner_count).astype(jnp.int32)
        tokens = jnp.repeat(jnp.arange(owner_count, dtype=jnp.int32), CAP)
        shuffle = jax.random.permutation(key_rest, owner_count * CAP).astype(jnp.int32)
        priority = jnp.where(tokens == fullest, shuffle - owner_count * CAP, shuffle)
        chosen = tokens[jnp.argsort(priority)[:PPD]]
        return chosen[jax.random.permutation(key_order, PPD)]
    block_keys = jax.random.split(jax.random.fold_in(key, 11), N_CTX)
    owners = jax.vmap(block_owners)(block_keys)
    onehot = (owners[..., None] == jnp.arange(owner_count, dtype=jnp.int32)).astype(jnp.int32)
    counted = jnp.cumsum(onehot, axis=1)
    page_rank = jnp.sum(counted * onehot, axis=-1) - 1

    def permute_slots(owner_key):
        return jax.random.permutation(owner_key, POOL_DEV).astype(jnp.int32)
    owner_keys = jax.random.split(jax.random.fold_in(key, 23), owner_count)
    slot_perm = jax.vmap(permute_slots)(owner_keys)
    local_slot = jnp.arange(N_CTX, dtype=jnp.int32)[:, None] * CAP + page_rank
    pool_slots = slot_perm[owners, local_slot]
    return (owners * POOL_DEV + pool_slots).reshape(-1).astype(jnp.int32)


def set_ends(array, key, least, high):
    place = [jax.random.randint(jax.random.fold_in(key, axis), (), 0, length) for axis, length in enumerate(array.shape)]
    main_axis = array.shape.index(max(array.shape))
    next_to = place[:main_axis] + [(place[main_axis] + 1) % array.shape[main_axis]] + place[main_axis + 1:]
    return array.at[tuple(place)].set(least).at[tuple(next_to)].set(high)


def steps_of(rng, dims, shards, least, high):
    factor_of, own = 1.0, jax.random.fold_in(rng, 6)
    for dim, shards_of in shards:
        heights = jnp.exp(jax.random.uniform(jax.random.fold_in(own, dim), (shards_of,), jnp.float32, least / len(shards), high / len(shards)))
        factor_of = factor_of * jnp.repeat(heights, dims[dim] // shards_of).reshape([-1 if axis == dim else 1 for axis in range(len(dims))])
    return factor_of


def normal_values(rng, dims, scale, most, cuts=(), kind=jnp.bfloat16):
    level = steps_of(rng, dims, cuts, -0.22, 0.18) if cuts else 1.0
    values = jax.random.normal(rng, dims, jnp.float32) * scale * level
    return jnp.minimum(jnp.maximum(values, -most), most).astype(kind)


def setup_inputs(seed: int = 0, part: int = 0) -> dict:
    splits = jax.random.split(jax.random.key(seed), 9)
    part_splits = jax.random.split(jax.random.fold_in(splits[8], part), 9)
    window_input = normal_values(part_splits[0], (WIN, D), 1.0, 6.0, ((0, 8), (1, 8)))
    gate_values = normal_values(part_splits[1], (WIN, D), 1.0, 6.0, ((0, 8), (1, 8)))
    page_pool = normal_values(part_splits[2], (POOL, PAGE, D), 1.0, 6.0, ((0, 64),))
    page_table = draw_page_table(jax.random.fold_in(jax.random.fold_in(splits[8], part), 71), part)
    filter_len = set_ends(jax.random.randint(splits[4], (D,), CACHE // 4, CACHE + 1), jax.random.fold_in(splits[4], 1), CACHE // 4, CACHE).astype(jnp.int32)
    residues = normal_values(splits[5], (D, MODES), 0.01, 0.06, ((0, 8),), jnp.float32)
    decays = jnp.clip(jnp.exp(math.log(0.1) - 6.9077553 * jax.random.uniform(splits[6], (D, MODES), jnp.float32) ** steps_of(splits[6], (D, MODES), ((0, 8),), -0.2, 0.2)), 0.0001, 0.1)
    skip_gain = jnp.clip(1.0 + 0.1 * jax.random.normal(splits[7], (D,), jnp.float32), 0.5, 1.5)
    return {"window_input": window_input, "gate_values": gate_values, "page_pool": page_pool, "page_table": page_table, "filter_len": filter_len, "residues": residues, "decays": decays, "skip_gain": skip_gain}


def reference(window_input, gate_values, page_pool, page_table, filter_len, residues, decays, skip_gain):
    cache = page_pool[page_table].reshape(CACHE, D)
    signal = jnp.concatenate([cache, window_input], axis=0)
    group_width = 256 if D % 256 == 0 else D
    group_count = D // group_width

    def one_group(group_index):
        first = group_index * group_width
        segment = lax.dynamic_slice_in_dim(signal, first, group_width, 1).astype(jnp.float32)
        decay_rate = lax.dynamic_slice_in_dim(decays, first, group_width, 0)
        weight = lax.dynamic_slice_in_dim(residues, first, group_width, 0)
        length = lax.dynamic_slice_in_dim(filter_len, first, group_width, 0)
        gate_part = lax.dynamic_slice_in_dim(gate_values, first, group_width, 1).astype(jnp.float32)
        skip_part = lax.dynamic_slice_in_dim(skip_gain, first, group_width, 0)
        positions = jnp.arange(SEQ, dtype=jnp.float32)
        filter_taps = jnp.sum(weight[None] * jnp.exp(-decay_rate[None] * positions[:, None, None]), axis=-1)
        in_reach = jnp.arange(SEQ, dtype=jnp.int32)[:, None] < length[None, :]
        filter_taps = jnp.where(in_reach, filter_taps, jnp.zeros_like(filter_taps))
        spectrum = jnp.fft.rfft(segment, axis=0) * jnp.fft.rfft(filter_taps, axis=0)
        convolved = jnp.fft.irfft(spectrum, n=SEQ, axis=0)[CACHE:]
        result = gate_part * (convolved + skip_part[None, :] * segment[CACHE:])
        return result.astype(jnp.bfloat16)

    outputs = lax.map(one_group, jnp.arange(group_count, dtype=jnp.int32))
    return jnp.transpose(outputs, (1, 0, 2)).reshape(WIN, D)
```

```python
import functools

import jax
import jax.numpy as jnp
from jax import lax
from jax.experimental import pallas as pl
from jax.experimental.pallas import tpu as pltpu
from jax.sharding import PartitionSpec as P

LANES = 128
SUBS = 8
VMEM_LIMIT = 32 * 1024 * 1024


def row(ref, index):
    return jnp.broadcast_to(ref[index : index + 1, :], (SUBS, LANES))


def shift_down(value, count):
    moved = pltpu.roll(value, count, 0)
    rows = lax.broadcasted_iota(jnp.int32, value.shape, 0)
    return jnp.where(rows >= count, moved, 0.0)


def segment_states(read, steps, lam):
    def body(step, states):
        value = read(step)
        return tuple(s * l + value for s, l in zip(states, lam))

    zero = jnp.zeros((SUBS, LANES), jnp.float32)
    return lax.fori_loop(0, steps, body, tuple(zero for _ in lam), unroll=4)


def exclusive_scan(end, decay, steps):
    total = end
    for count in (1, 2, 4):
        total = total + jnp.exp(-decay * float(steps * count)) * shift_down(total, count)
    return shift_down(total, 1)


def segment_outputs(read, write, steps, lam, gain, begin):
    def body(step, states):
        value = read(step)
        new = tuple(s * l + g * value for s, l, g in zip(states, lam, gain))
        parts = list(new)
        while len(parts) > 1:
            parts = [a + b for a, b in zip(parts[::2], parts[1::2])]
        write(step, parts[0])
        return new

    lax.fori_loop(0, steps, body, tuple(begin), unroll=4)


def window_kernel(modes, steps, window_ref, decay_ref, weight_ref, out_ref, signal):
    signal[...] = window_ref[...].astype(jnp.float32)
    decay = [row(decay_ref, r) for r in range(modes)]
    lam = [jnp.exp(-d) for d in decay]

    def read(step):
        return signal[pl.ds(step, SUBS, stride=steps), :]

    def write(step, value):
        out_ref[pl.ds(step, SUBS, stride=steps), :] = value

    ends = segment_states(read, steps, lam)
    gain = [row(weight_ref, r) for r in range(modes)]
    begin = [
        gain[r] * exclusive_scan(ends[r], row(decay_ref, r), steps) for r in range(modes)
    ]
    segment_outputs(read, write, steps, lam, gain, begin)


def cache_kernel(
    modes,
    steps,
    slots_ref,
    pages_ref,
    length_ref,
    decay_ref,
    weight_ref,
    window_part_ref,
    out_ref,
    signal,
    result,
):
    page_count = slots_ref.shape[0]
    cached = page_count * SUBS
    rows = lax.broadcasted_iota(jnp.int32, (SUBS, LANES), 0)
    length = jnp.broadcast_to(length_ref[...], (SUBS, LANES))
    first = cached - length

    lam_page = [jnp.exp(-float(SUBS) * row(decay_ref, r)) for r in range(modes)]

    def scan_page(page, states):
        value = pages_ref[slots_ref[page]].astype(jnp.float32)
        start = pl.multiple_of(page * SUBS, SUBS)
        signal[pl.ds(start, SUBS), :] = value
        value = jnp.where(rows + page * SUBS > first, value, 0.0)
        return tuple(s * l + value for s, l in zip(states, lam_page))

    zero = jnp.zeros((SUBS, LANES), jnp.float32)
    states = lax.fori_loop(0, page_count, scan_page, tuple(zero for _ in range(modes)), unroll=4)
    rows_float = rows.astype(jnp.float32)
    history = []
    for r in range(modes):
        decay = row(decay_ref, r)
        weighted = states[r] * jnp.exp(-decay * (float(SUBS - 1) - rows_float))
        total = jnp.sum(weighted, axis=0, keepdims=True)
        history.append(jnp.broadcast_to(total, (SUBS, LANES)) * row(weight_ref, r))

    window = steps * SUBS
    shift = cached // 2
    reach = cached - window
    while shift >= 1:
        keep = window + min(shift - 1, reach) if shift > 1 else window
        keep = min(keep, cached - shift)
        size = 128 if shift >= 128 else 64 if shift >= 64 else 32 if shift >= 32 else 16 if shift >= 16 else 8
        chunk = min(size, 64)
        count = -(-keep // chunk)
        wide = (jnp.broadcast_to(first[0:1, :], (chunk, LANES)) & shift) != 0

        def move(index, carry, chunk=chunk, wide=wide, shift=shift):
            start = pl.multiple_of(index * chunk, chunk)
            near = signal[pl.ds(start, chunk), :]
            far = signal[pl.ds(start + shift, chunk), :]
            signal[pl.ds(start, chunk), :] = jnp.where(wide, far, near)
            return carry

        lax.fori_loop(0, count, move, 0)
        shift //= 2
    signal[0:SUBS, :] = jnp.where(rows > 0, signal[0:SUBS, :], 0.0)

    lam = [jnp.exp(-row(decay_ref, r)) for r in range(modes)]

    def read(step):
        return signal[pl.ds(step, SUBS, stride=steps), :]

    def write(step, value):
        result[pl.ds(step, SUBS, stride=steps), :] = value

    ends = segment_states(read, steps, lam)
    length_float = length.astype(jnp.float32)
    gain = [
        -row(weight_ref, r) * jnp.exp(-row(decay_ref, r) * length_float) for r in range(modes)
    ]
    begin = []
    for r in range(modes):
        decay = row(decay_ref, r)
        from_cache = history[r] * jnp.exp(-decay * (float(steps) * rows_float))
        begin.append(from_cache + gain[r] * exclusive_scan(ends[r], decay, steps))
    segment_outputs(read, write, steps, lam, gain, begin)
    out_ref[...] = (result[...] + window_part_ref[...]).astype(jnp.bfloat16)


def gate_kernel(conv_ref, window_ref, gate_ref, skip_ref, out_ref):
    for block in range(conv_ref.shape[0]):
        lanes = slice(block * LANES, (block + 1) * LANES)
        mixed = conv_ref[block].astype(jnp.float32) + skip_ref[:, lanes] * window_ref[
            :, lanes
        ].astype(jnp.float32)
        out_ref[:, lanes] = (gate_ref[:, lanes].astype(jnp.float32) * mixed).astype(jnp.bfloat16)


def vmem(count):
    return [pl.BlockSpec(memory_space=pltpu.VMEM) for _ in range(count)]


def params():
    return pltpu.CompilerParams(vmem_limit_bytes=VMEM_LIMIT)


def window_conv(window_seq, decay, weight):
    window = window_seq.shape[0]
    modes = decay.shape[0]
    return pl.pallas_call(
        functools.partial(window_kernel, modes, window // SUBS),
        out_shape=jax.ShapeDtypeStruct((window, LANES), jnp.float32),
        in_specs=vmem(3),
        out_specs=pl.BlockSpec(memory_space=pltpu.VMEM),
        scratch_shapes=[pltpu.VMEM((window, LANES), jnp.float32)],
        compiler_params=params(),
        cost_estimate=pl.CostEstimate(
            flops=12 * window * LANES * modes, bytes_accessed=6 * window * LANES, transcendentals=0
        ),
        name="window_conv",
    )(window_seq, decay, weight)


def cache_conv(slots, pages, length, decay, weight, window_part):
    window = window_part.shape[0]
    modes = decay.shape[0]
    cached = slots.shape[0] * SUBS
    return pl.pallas_call(
        functools.partial(cache_kernel, modes, window // SUBS),
        out_shape=jax.ShapeDtypeStruct((window, LANES), jnp.bfloat16),
        in_specs=[pl.BlockSpec(memory_space=pltpu.SMEM)] + vmem(5),
        out_specs=pl.BlockSpec(memory_space=pltpu.VMEM),
        scratch_shapes=[
            pltpu.VMEM((cached + 64, LANES), jnp.float32),
            pltpu.VMEM((window, LANES), jnp.float32),
        ],
        compiler_params=params(),
        cost_estimate=pl.CostEstimate(
            flops=4 * cached * LANES * modes, bytes_accessed=4 * cached * LANES, transcendentals=0
        ),
        name="cache_conv",
    )(slots, pages, length, decay, weight, window_part)


def gate_out(conv_home, window_input, gate_values, skip_gain):
    return pl.pallas_call(
        gate_kernel,
        out_shape=jax.ShapeDtypeStruct(gate_values.shape, jnp.bfloat16),
        in_specs=vmem(4),
        out_specs=pl.BlockSpec(memory_space=pltpu.VMEM),
        compiler_params=params(),
        name="gate_out",
    )(conv_home, window_input, gate_values, skip_gain)


def local(
    window_input, gate_values, page_pool, page_table, filter_len, residues, decays, skip_gain
):
    ctx_count = lax.axis_size("ctx")
    chan_count = lax.axis_size("chan")
    ctx_pos = lax.axis_index("ctx")
    pool_pages, page_len, width = page_pool.shape
    pencil = window_input.shape[1] // ctx_count
    parcel = jnp.transpose(page_pool.reshape(pool_pages, page_len, -1, pencil), (2, 0, 1, 3))
    arrived = lax.all_to_all(parcel, ("chan", "ctx"), split_axis=0, concat_axis=0, tiled=True)
    arrived = arrived.reshape(-1, page_len, pencil)
    window_seq = lax.all_to_all(window_input, "ctx", split_axis=1, concat_axis=0, tiled=True)
    owners = page_table // pool_pages
    source = (owners % chan_count) * ctx_count + owners // chan_count
    slots = source * pool_pages + page_table % pool_pages
    start = ctx_pos * pencil
    decay = lax.dynamic_slice_in_dim(decays, start, pencil, 0).T
    weight = lax.dynamic_slice_in_dim(residues, start, pencil, 0).T
    length = lax.dynamic_slice_in_dim(filter_len, start, pencil, 0)[None, :]
    window_part = window_conv(window_seq, decay, weight)
    convolved = cache_conv(slots, arrived, length, decay, weight, window_part)
    conv_home = lax.all_to_all(
        convolved.reshape(ctx_count, -1, pencil), "ctx", split_axis=0, concat_axis=0, tiled=True
    )
    return gate_out(conv_home, window_input, gate_values, skip_gain[None, :])


def solution(mesh):
    in_specs = (
        P(("req", "ctx"), "chan"),
        P(("req", "ctx"), "chan"),
        P(("req", "ctx", "chan"), None, None),
        P("req"),
        P("chan"),
        P("chan", None),
        P("chan", None),
        P("chan"),
    )
    out_specs = P(("req", "ctx"), "chan")
    return jax.shard_map(local, mesh=mesh, in_specs=in_specs, out_specs=out_specs, check_vma=False)
```

```python
import functools

import jax
import jax.numpy as jnp
from jax import lax
from jax.experimental import pallas as pl
from jax.experimental.pallas import tpu as pltpu
from jax.sharding import PartitionSpec as P

LANES = 128
SUBS = 8
VMEM_LIMIT = 32 * 1024 * 1024


def row(ref, index):
    return jnp.broadcast_to(ref[index : index + 1, :], (SUBS, LANES))


def shift_down(value, count):
    moved = pltpu.roll(value, count, 0)
    rows = lax.broadcasted_iota(jnp.int32, value.shape, 0)
    return jnp.where(rows >= count, moved, 0.0)


def segment_states(read, steps, lam):
    def body(step, states):
        value = read(step)
        return tuple(s * l + value for s, l in zip(states, lam))

    zero = jnp.zeros((SUBS, LANES), jnp.float32)
    return lax.fori_loop(0, steps, body, tuple(zero for _ in lam), unroll=4)


def inclusive_scan(end, decay, steps):
    total = end
    for count in (1, 2, 4):
        total = total + jnp.exp(-decay * float(steps * count)) * shift_down(total, count)
    return total


def segment_outputs(read, write, steps, lam, gain, begin):
    def body(step, states):
        value = read(step)
        new = tuple(s * l + g * value for s, l, g in zip(states, lam, gain))
        parts = list(new)
        while len(parts) > 1:
            parts = [a + b for a, b in zip(parts[::2], parts[1::2])]
        write(step, parts[0])
        return new

    lax.fori_loop(0, steps, body, tuple(begin), unroll=4)


def window_kernel(modes, steps, window_ref, decay_ref, weight_ref, skip_ref, base_ref, end_ref, signal, result):
    tiles = window_ref.shape[1] // LANES

    def tile(index, carry):
        lanes = pl.ds(pl.multiple_of(index * LANES, LANES), LANES)

        def wide(ref, r):
            return jnp.broadcast_to(ref[r : r + 1, lanes], (SUBS, LANES))

        signal[...] = window_ref[:, lanes].astype(jnp.float32)
        lam = [jnp.exp(-wide(decay_ref, r)) for r in range(modes)]
        skip = wide(skip_ref, 0)

        def read(step):
            return signal[pl.ds(step, SUBS, stride=steps), :]

        def write(step, value):
            result[pl.ds(step, SUBS, stride=steps), :] = value + skip * read(step)

        ends = segment_states(read, steps, lam)
        gain = [wide(weight_ref, r) for r in range(modes)]
        begin = []
        for r in range(modes):
            total = inclusive_scan(ends[r], wide(decay_ref, r), steps)
            end_ref[r : r + 1, lanes] = total[SUBS - 1 : SUBS, :]
            begin.append(gain[r] * shift_down(total, 1))
        segment_outputs(read, write, steps, lam, gain, begin)
        base_ref[:, lanes] = result[...]
        return carry

    lax.fori_loop(0, tiles, tile, 0)


def carry_kernel(modes, base_ref, state_ref, decay_ref, weight_ref, out_ref):
    tiles = base_ref.shape[1] // LANES
    ahead = lax.broadcasted_iota(jnp.int32, (SUBS, LANES), 0).astype(jnp.float32) + 1.0

    def tile(index, carry):
        lanes = pl.ds(pl.multiple_of(index * LANES, LANES), LANES)

        def wide(ref, r):
            return jnp.broadcast_to(ref[r : r + 1, lanes], (SUBS, LANES))

        term = [
            wide(weight_ref, r) * wide(state_ref, r) * jnp.exp(-wide(decay_ref, r) * ahead)
            for r in range(modes)
        ]
        lam = [jnp.exp(-float(SUBS) * wide(decay_ref, r)) for r in range(modes)]
        for first in range(0, base_ref.shape[0], SUBS):
            parts = list(term)
            while len(parts) > 1:
                parts = [a + b for a, b in zip(parts[::2], parts[1::2])]
            out_ref[first : first + SUBS, lanes] = base_ref[first : first + SUBS, lanes] + parts[0]
            term = [t * l for t, l in zip(term, lam)]
        return carry

    lax.fori_loop(0, tiles, tile, 0)


def cache_kernel(
    modes,
    steps,
    slots_ref,
    pages_ref,
    length_ref,
    decay_ref,
    weight_ref,
    out_ref,
    signal,
    result,
):
    page_count = slots_ref.shape[0]
    cached = page_count * SUBS
    rows = lax.broadcasted_iota(jnp.int32, (SUBS, LANES), 0)
    length = jnp.broadcast_to(length_ref[...], (SUBS, LANES))
    first = cached - length

    lam_page = [jnp.exp(-float(SUBS) * row(decay_ref, r)) for r in range(modes)]

    def scan_page(page, states):
        value = pages_ref[slots_ref[page]].astype(jnp.float32)
        start = pl.multiple_of(page * SUBS, SUBS)
        signal[pl.ds(start, SUBS), :] = value
        value = jnp.where(rows + page * SUBS > first, value, 0.0)
        return tuple(s * l + value for s, l in zip(states, lam_page))

    zero = jnp.zeros((SUBS, LANES), jnp.float32)
    states = lax.fori_loop(0, page_count, scan_page, tuple(zero for _ in range(modes)), unroll=4)
    rows_float = rows.astype(jnp.float32)
    history = []
    for r in range(modes):
        decay = row(decay_ref, r)
        weighted = states[r] * jnp.exp(-decay * (float(SUBS - 1) - rows_float))
        total = jnp.sum(weighted, axis=0, keepdims=True)
        history.append(jnp.broadcast_to(total, (SUBS, LANES)) * row(weight_ref, r))

    window = steps * SUBS
    shift = cached // 2
    reach = cached - window
    while shift >= 1:
        keep = window + min(shift - 1, reach) if shift > 1 else window
        keep = min(keep, cached - shift)
        size = 128 if shift >= 128 else 64 if shift >= 64 else 32 if shift >= 32 else 16 if shift >= 16 else 8
        chunk = min(size, 64)
        count = -(-keep // chunk)
        wide = (jnp.broadcast_to(first[0:1, :], (chunk, LANES)) & shift) != 0

        def move(index, carry, chunk=chunk, wide=wide, shift=shift):
            start = pl.multiple_of(index * chunk, chunk)
            near = signal[pl.ds(start, chunk), :]
            far = signal[pl.ds(start + shift, chunk), :]
            signal[pl.ds(start, chunk), :] = jnp.where(wide, far, near)
            return carry

        lax.fori_loop(0, count, move, 0)
        shift //= 2
    signal[0:SUBS, :] = jnp.where(rows > 0, signal[0:SUBS, :], 0.0)

    lam = [jnp.exp(-row(decay_ref, r)) for r in range(modes)]

    def read(step):
        return signal[pl.ds(step, SUBS, stride=steps), :]

    def write(step, value):
        result[pl.ds(step, SUBS, stride=steps), :] = value

    ends = segment_states(read, steps, lam)
    length_float = length.astype(jnp.float32)
    gain = [
        -row(weight_ref, r) * jnp.exp(-row(decay_ref, r) * length_float) for r in range(modes)
    ]
    begin = []
    for r in range(modes):
        decay = row(decay_ref, r)
        from_cache = history[r] * jnp.exp(-decay * (float(steps) * rows_float))
        begin.append(from_cache + gain[r] * shift_down(inclusive_scan(ends[r], decay, steps), 1))
    segment_outputs(read, write, steps, lam, gain, begin)
    out_ref[...] = result[...].astype(jnp.bfloat16)


def gate_kernel(conv_ref, base_ref, gate_ref, out_ref):
    for block in range(conv_ref.shape[0]):
        lanes = slice(block * LANES, (block + 1) * LANES)
        mixed = conv_ref[block].astype(jnp.float32) + base_ref[:, lanes]
        out_ref[:, lanes] = (gate_ref[:, lanes].astype(jnp.float32) * mixed).astype(jnp.bfloat16)


def vmem(count):
    return [pl.BlockSpec(memory_space=pltpu.VMEM) for _ in range(count)]


def params():
    return pltpu.CompilerParams(vmem_limit_bytes=VMEM_LIMIT)


def window_conv(window, decay, weight, skip):
    rows, width = window.shape
    modes = decay.shape[0]
    return pl.pallas_call(
        functools.partial(window_kernel, modes, rows // SUBS),
        out_shape=(
            jax.ShapeDtypeStruct((rows, width), jnp.float32),
            jax.ShapeDtypeStruct((modes, width), jnp.float32),
        ),
        in_specs=vmem(4),
        out_specs=tuple(vmem(2)),
        scratch_shapes=[pltpu.VMEM((rows, LANES), jnp.float32)] * 2,
        compiler_params=params(),
        cost_estimate=pl.CostEstimate(
            flops=12 * rows * width * modes, bytes_accessed=6 * rows * width, transcendentals=0
        ),
        name="window_conv",
    )(window, decay, weight, skip)


def add_carry(base, state, decay, weight):
    rows, width = base.shape
    modes = decay.shape[0]
    return pl.pallas_call(
        functools.partial(carry_kernel, modes),
        out_shape=jax.ShapeDtypeStruct((rows, width), jnp.float32),
        in_specs=vmem(4),
        out_specs=pl.BlockSpec(memory_space=pltpu.VMEM),
        compiler_params=params(),
        cost_estimate=pl.CostEstimate(
            flops=3 * rows * width * modes, bytes_accessed=8 * rows * width, transcendentals=0
        ),
        name="add_carry",
    )(base, state, decay, weight)


def cache_conv(slots, pages, length, decay, weight, window):
    modes = decay.shape[0]
    cached = slots.shape[0] * SUBS
    return pl.pallas_call(
        functools.partial(cache_kernel, modes, window // SUBS),
        out_shape=jax.ShapeDtypeStruct((window, LANES), jnp.bfloat16),
        in_specs=[pl.BlockSpec(memory_space=pltpu.SMEM)] + vmem(4),
        out_specs=pl.BlockSpec(memory_space=pltpu.VMEM),
        scratch_shapes=[
            pltpu.VMEM((cached + 64, LANES), jnp.float32),
            pltpu.VMEM((window, LANES), jnp.float32),
        ],
        compiler_params=params(),
        cost_estimate=pl.CostEstimate(
            flops=4 * cached * LANES * modes, bytes_accessed=4 * cached * LANES, transcendentals=0
        ),
        name="cache_conv",
    )(slots, pages, length, decay, weight)


def gate_out(conv_home, base, gate_values):
    return pl.pallas_call(
        gate_kernel,
        out_shape=jax.ShapeDtypeStruct(gate_values.shape, jnp.bfloat16),
        in_specs=vmem(3),
        out_specs=pl.BlockSpec(memory_space=pltpu.VMEM),
        compiler_params=params(),
        name="gate_out",
    )(conv_home, base, gate_values)


def start_states(ends, decay, rows, count):
    state = lax.ppermute(ends, "ctx", [(i, i + 1) for i in range(count - 1)])
    hop = 1
    while hop < count:
        before = lax.ppermute(state, "ctx", [(i, i + hop) for i in range(count - hop)])
        state = state + jnp.exp(-decay * float(rows * hop)) * before
        hop *= 2
    return state


def local(
    window_input, gate_values, page_pool, page_table, filter_len, residues, decays, skip_gain
):
    ctx_count = lax.axis_size("ctx")
    chan_count = lax.axis_size("chan")
    ctx_pos = lax.axis_index("ctx")
    pool_pages, page_len, width = page_pool.shape
    rows = window_input.shape[0]
    pencil = window_input.shape[1] // ctx_count
    parcel = jnp.transpose(page_pool.reshape(pool_pages, page_len, -1, pencil), (2, 0, 1, 3))
    arrived = lax.all_to_all(parcel, ("chan", "ctx"), split_axis=0, concat_axis=0, tiled=True)
    arrived = arrived.reshape(-1, page_len, pencil)
    owners = page_table // pool_pages
    source = (owners % chan_count) * ctx_count + owners // chan_count
    slots = source * pool_pages + page_table % pool_pages
    start = ctx_pos * pencil
    decay = lax.dynamic_slice_in_dim(decays, start, pencil, 0).T
    weight = lax.dynamic_slice_in_dim(residues, start, pencil, 0).T
    length = lax.dynamic_slice_in_dim(filter_len, start, pencil, 0)[None, :]
    base, ends = window_conv(window_input, decays.T, residues.T, skip_gain[None, :])
    state = start_states(ends, decays.T, rows, ctx_count)
    base = add_carry(base, state, decays.T, residues.T)
    convolved = cache_conv(slots, arrived, length, decay, weight, rows * ctx_count)
    conv_home = lax.all_to_all(
        convolved.reshape(ctx_count, -1, pencil), "ctx", split_axis=0, concat_axis=0, tiled=True
    )
    return gate_out(conv_home, base, gate_values)


def solution(mesh):
    in_specs = (
        P(("req", "ctx"), "chan"),
        P(("req", "ctx"), "chan"),
        P(("req", "ctx", "chan"), None, None),
        P("req"),
        P("chan"),
        P("chan", None),
        P("chan", None),
        P("chan"),
    )
    out_specs = P(("req", "ctx"), "chan")
    return jax.shard_map(local, mesh=mesh, in_specs=in_specs, out_specs=out_specs, check_vma=False)
```

```python
import functools

import jax
import jax.numpy as jnp
from jax import lax
from jax.experimental import pallas as pl
from jax.experimental.pallas import tpu as pltpu
from jax.sharding import PartitionSpec as P

LANES = 128
SUBS = 8
VMEM_LIMIT = 32 * 1024 * 1024


def row(ref, index):
    return jnp.broadcast_to(ref[index : index + 1, :], (SUBS, LANES))


def shift_down(value, count):
    moved = pltpu.roll(value, count, 0)
    rows = lax.broadcasted_iota(jnp.int32, value.shape, 0)
    return jnp.where(rows >= count, moved, 0.0)


def segment_states(read, steps, lam):
    def body(step, states):
        value = read(step)
        return tuple(s * l + value for s, l in zip(states, lam))

    zero = jnp.zeros((SUBS, LANES), jnp.float32)
    return lax.fori_loop(0, steps, body, tuple(zero for _ in lam), unroll=4)


def inclusive_scan(end, decay, steps):
    total = end
    for count in (1, 2, 4):
        total = total + jnp.exp(-decay * float(steps * count)) * shift_down(total, count)
    return total


def segment_outputs(read, write, steps, lam, gain, begin):
    def body(step, states):
        value = read(step)
        new = tuple(s * l + g * value for s, l, g in zip(states, lam, gain))
        parts = list(new)
        while len(parts) > 1:
            parts = [a + b for a, b in zip(parts[::2], parts[1::2])]
        write(step, parts[0])
        return new

    lax.fori_loop(0, steps, body, tuple(begin), unroll=4)


def window_kernel(modes, steps, window_ref, decay_ref, weight_ref, skip_ref, base_ref, end_ref, signal, result):
    tiles = window_ref.shape[1] // LANES

    def tile(index, carry):
        lanes = pl.ds(pl.multiple_of(index * LANES, LANES), LANES)

        def wide(ref, r):
            return jnp.broadcast_to(ref[r : r + 1, lanes], (SUBS, LANES))

        signal[...] = window_ref[:, lanes].astype(jnp.float32)
        lam = [jnp.exp(-wide(decay_ref, r)) for r in range(modes)]
        skip = wide(skip_ref, 0)

        def read(step):
            return signal[pl.ds(step, SUBS, stride=steps), :]

        def write(step, value):
            result[pl.ds(step, SUBS, stride=steps), :] = value + skip * read(step)

        ends = segment_states(read, steps, lam)
        gain = [wide(weight_ref, r) for r in range(modes)]
        begin = []
        for r in range(modes):
            total = inclusive_scan(ends[r], wide(decay_ref, r), steps)
            end_ref[r : r + 1, lanes] = total[SUBS - 1 : SUBS, :]
            begin.append(gain[r] * shift_down(total, 1))
        segment_outputs(read, write, steps, lam, gain, begin)
        base_ref[:, lanes] = result[...]
        return carry

    lax.fori_loop(0, tiles, tile, 0)


def cache_kernel(
    modes,
    steps,
    place_ref,
    slots_ref,
    pages_ref,
    length_ref,
    decay_ref,
    weight_ref,
    *rest,
):
    end_refs, (out_ref, signal, result, before) = rest[:SUBS], rest[SUBS:]
    for hop, end_ref in enumerate(end_refs):
        segment = lax.rem(place_ref[0] + (SUBS - hop), SUBS)
        before[pl.ds(segment, modes, stride=SUBS), :] = end_ref[...]
    page_count = slots_ref.shape[0]
    cached = page_count * SUBS
    rows = lax.broadcasted_iota(jnp.int32, (SUBS, LANES), 0)
    length = jnp.broadcast_to(length_ref[...], (SUBS, LANES))
    first = cached - length

    lam_page = [jnp.exp(-float(SUBS) * row(decay_ref, r)) for r in range(modes)]

    def scan_page(page, states):
        value = pages_ref[slots_ref[page]].astype(jnp.float32)
        start = pl.multiple_of(page * SUBS, SUBS)
        signal[pl.ds(start, SUBS), :] = value
        value = jnp.where(rows + page * SUBS > first, value, 0.0)
        return tuple(s * l + value for s, l in zip(states, lam_page))

    zero = jnp.zeros((SUBS, LANES), jnp.float32)
    states = lax.fori_loop(0, page_count, scan_page, tuple(zero for _ in range(modes)), unroll=4)
    rows_float = rows.astype(jnp.float32)
    history = []
    for r in range(modes):
        decay = row(decay_ref, r)
        weighted = states[r] * jnp.exp(-decay * (float(SUBS - 1) - rows_float))
        total = jnp.sum(weighted, axis=0, keepdims=True)
        history.append(jnp.broadcast_to(total, (SUBS, LANES)) * row(weight_ref, r))

    window = steps * SUBS
    shift = cached // 2
    reach = cached - window
    while shift >= 1:
        keep = window + min(shift - 1, reach) if shift > 1 else window
        keep = min(keep, cached - shift)
        size = 128 if shift >= 128 else 64 if shift >= 64 else 32 if shift >= 32 else 16 if shift >= 16 else 8
        chunk = min(size, 64)
        count = -(-keep // chunk)
        wide = (jnp.broadcast_to(first[0:1, :], (chunk, LANES)) & shift) != 0

        def move(index, carry, chunk=chunk, wide=wide, shift=shift):
            start = pl.multiple_of(index * chunk, chunk)
            near = signal[pl.ds(start, chunk), :]
            far = signal[pl.ds(start + shift, chunk), :]
            signal[pl.ds(start, chunk), :] = jnp.where(wide, far, near)
            return carry

        lax.fori_loop(0, count, move, 0)
        shift //= 2
    signal[0:SUBS, :] = jnp.where(rows > 0, signal[0:SUBS, :], 0.0)

    lam = [jnp.exp(-row(decay_ref, r)) for r in range(modes)]

    def read(step):
        return signal[pl.ds(step, SUBS, stride=steps), :]

    def write(step, value):
        result[pl.ds(step, SUBS, stride=steps), :] = value

    ends = segment_states(read, steps, lam)
    length_float = length.astype(jnp.float32)
    gain = [
        -row(weight_ref, r) * jnp.exp(-row(decay_ref, r) * length_float) for r in range(modes)
    ]
    begin = []
    for r in range(modes):
        decay = row(decay_ref, r)
        from_cache = history[r] * jnp.exp(-decay * (float(steps) * rows_float))
        prior = inclusive_scan(before[r * SUBS : (r + 1) * SUBS, :], decay, steps)
        from_cache = from_cache + row(weight_ref, r) * shift_down(prior, 1)
        begin.append(from_cache + gain[r] * shift_down(inclusive_scan(ends[r], decay, steps), 1))
    segment_outputs(read, write, steps, lam, gain, begin)
    out_ref[...] = result[...].astype(jnp.bfloat16)


def gate_kernel(conv_ref, base_ref, gate_ref, out_ref):
    for block in range(conv_ref.shape[0]):
        lanes = slice(block * LANES, (block + 1) * LANES)
        mixed = conv_ref[block].astype(jnp.float32) + base_ref[:, lanes]
        out_ref[:, lanes] = (gate_ref[:, lanes].astype(jnp.float32) * mixed).astype(jnp.bfloat16)


def vmem(count):
    return [pl.BlockSpec(memory_space=pltpu.VMEM) for _ in range(count)]


def params():
    return pltpu.CompilerParams(vmem_limit_bytes=VMEM_LIMIT)


def window_conv(window, decay, weight, skip):
    rows, width = window.shape
    modes = decay.shape[0]
    return pl.pallas_call(
        functools.partial(window_kernel, modes, rows // SUBS),
        out_shape=(
            jax.ShapeDtypeStruct((rows, width), jnp.float32),
            jax.ShapeDtypeStruct((modes, width), jnp.float32),
        ),
        in_specs=vmem(4),
        out_specs=tuple(vmem(2)),
        scratch_shapes=[pltpu.VMEM((rows, LANES), jnp.float32)] * 2,
        compiler_params=params(),
        cost_estimate=pl.CostEstimate(
            flops=12 * rows * width * modes, bytes_accessed=6 * rows * width, transcendentals=0
        ),
        name="window_conv",
    )(window, decay, weight, skip)


def cache_conv(place, slots, pages, length, decay, weight, ends, window):
    modes = decay.shape[0]
    cached = slots.shape[0] * SUBS
    return pl.pallas_call(
        functools.partial(cache_kernel, modes, window // SUBS),
        out_shape=jax.ShapeDtypeStruct((window, LANES), jnp.bfloat16),
        in_specs=[pl.BlockSpec(memory_space=pltpu.SMEM)] * 2 + vmem(4 + len(ends)),
        out_specs=pl.BlockSpec(memory_space=pltpu.VMEM),
        scratch_shapes=[
            pltpu.VMEM((cached + 64, LANES), jnp.float32),
            pltpu.VMEM((window, LANES), jnp.float32),
            pltpu.VMEM((modes * SUBS, LANES), jnp.float32),
        ],
        compiler_params=params(),
        cost_estimate=pl.CostEstimate(
            flops=4 * cached * LANES * modes, bytes_accessed=4 * cached * LANES, transcendentals=0
        ),
        name="cache_conv",
    )(place, slots, pages, length, decay, weight, *ends)


def gate_out(conv_home, base, gate_values):
    return pl.pallas_call(
        gate_kernel,
        out_shape=jax.ShapeDtypeStruct(gate_values.shape, jnp.bfloat16),
        in_specs=vmem(3),
        out_specs=pl.BlockSpec(memory_space=pltpu.VMEM),
        compiler_params=params(),
        name="gate_out",
    )(conv_home, base, gate_values)


def end_states(ends, place, count):
    pencil = ends.shape[1] // count

    def block(hop):
        return lax.dynamic_slice_in_dim(ends, (place + hop) % count * pencil, pencil, 1)

    return [block(0)] + [
        lax.ppermute(block(hop), "ctx", [(i, (i + hop) % count) for i in range(count)])
        for hop in range(1, count)
    ]


def local(
    window_input, gate_values, page_pool, page_table, filter_len, residues, decays, skip_gain
):
    ctx_count = lax.axis_size("ctx")
    chan_count = lax.axis_size("chan")
    ctx_pos = lax.axis_index("ctx")
    pool_pages, page_len, width = page_pool.shape
    rows = window_input.shape[0]
    pencil = window_input.shape[1] // ctx_count
    parcel = jnp.transpose(page_pool.reshape(pool_pages, page_len, -1, pencil), (2, 0, 1, 3))
    arrived = lax.all_to_all(parcel, ("chan", "ctx"), split_axis=0, concat_axis=0, tiled=True)
    arrived = arrived.reshape(-1, page_len, pencil)
    owners = page_table // pool_pages
    source = (owners % chan_count) * ctx_count + owners // chan_count
    slots = source * pool_pages + page_table % pool_pages
    start = ctx_pos * pencil
    decay = lax.dynamic_slice_in_dim(decays, start, pencil, 0).T
    weight = lax.dynamic_slice_in_dim(residues, start, pencil, 0).T
    length = lax.dynamic_slice_in_dim(filter_len, start, pencil, 0)[None, :]
    base, ends = window_conv(window_input, decays.T, residues.T, skip_gain[None, :])
    ends = end_states(ends, ctx_pos, ctx_count)
    convolved = cache_conv(
        ctx_pos[None], slots, arrived, length, decay, weight, ends, rows * ctx_count
    )
    conv_home = lax.all_to_all(
        convolved.reshape(ctx_count, -1, pencil), "ctx", split_axis=0, concat_axis=0, tiled=True
    )
    return gate_out(conv_home, base, gate_values)


def solution(mesh):
    in_specs = (
        P(("req", "ctx"), "chan"),
        P(("req", "ctx"), "chan"),
        P(("req", "ctx", "chan"), None, None),
        P("req"),
        P("chan"),
        P("chan", None),
        P("chan", None),
        P("chan"),
    )
    out_specs = P(("req", "ctx"), "chan")
    return jax.shard_map(local, mesh=mesh, in_specs=in_specs, out_specs=out_specs, check_vma=False)
```

```python
import functools

import jax
import jax.numpy as jnp
from jax import lax
from jax.experimental import pallas as pl
from jax.experimental.pallas import tpu as pltpu
from jax.sharding import PartitionSpec as P

LANES = 128
SUBS = 8
RANKS = 2
KEPT = 3
CHUNK = 64
VMEM_LIMIT = 16 * 1024 * 1024


def row(ref, index):
    return jnp.broadcast_to(ref[index : index + 1, :], (SUBS, LANES))


def shift_down(value, count):
    moved = pltpu.roll(value, count, 0)
    rows = lax.broadcasted_iota(jnp.int32, value.shape, 0)
    return jnp.where(rows >= count, moved, 0.0)


def segment_states(read, steps, lam):
    def body(step, states):
        value = read(step)
        return tuple(s * l + value for s, l in zip(states, lam))

    zero = jnp.zeros((SUBS, LANES), jnp.float32)
    return lax.fori_loop(0, steps, body, tuple(zero for _ in lam), unroll=4)


def inclusive_scan(end, decay, steps):
    total = end
    for count in (1, 2, 4):
        total = total + jnp.exp(-decay * float(steps * count)) * shift_down(total, count)
    return total


def segment_outputs(read, write, steps, lam, gain, begin):
    def body(step, states):
        value = read(step)
        new = tuple(s * l + g * value for s, l, g in zip(states, lam, gain))
        parts = list(new)
        while len(parts) > 1:
            parts = [a + b for a, b in zip(parts[::2], parts[1::2])]
        write(step, parts[0])
        return new

    lax.fori_loop(0, steps, body, tuple(begin), unroll=4)


def window_kernel(modes, steps, window_ref, decay_ref, weight_ref, skip_ref, base_ref, end_ref, signal, result):
    tiles = window_ref.shape[1] // LANES

    def tile(index, carry):
        lanes = pl.ds(pl.multiple_of(index * LANES, LANES), LANES)

        def wide(ref, r):
            return jnp.broadcast_to(ref[r : r + 1, lanes], (SUBS, LANES))

        signal[...] = window_ref[:, lanes].astype(jnp.float32)
        lam = [jnp.exp(-wide(decay_ref, r)) for r in range(modes)]
        skip = wide(skip_ref, 0)

        def read(step):
            return signal[pl.ds(step, SUBS, stride=steps), :]

        def write(step, value):
            result[pl.ds(step, SUBS, stride=steps), :] = value + skip * read(step)

        ends = segment_states(read, steps, lam)
        gain = [wide(weight_ref, r) for r in range(modes)]
        begin = []
        for r in range(modes):
            total = inclusive_scan(ends[r], wide(decay_ref, r), steps)
            end_ref[r : r + 1, lanes] = total[SUBS - 1 : SUBS, :]
            begin.append(gain[r] * shift_down(total, 1))
        segment_outputs(read, write, steps, lam, gain, begin)
        base_ref[:, lanes] = result[...]
        return carry

    lax.fori_loop(0, tiles, tile, 0)


def carry_kernel(modes, base_ref, state_ref, decay_ref, weight_ref, out_ref):
    tiles = base_ref.shape[1] // LANES
    ahead = lax.broadcasted_iota(jnp.int32, (SUBS, LANES), 0).astype(jnp.float32) + 1.0

    def tile(index, carry):
        lanes = pl.ds(pl.multiple_of(index * LANES, LANES), LANES)

        def wide(ref, r):
            return jnp.broadcast_to(ref[r : r + 1, lanes], (SUBS, LANES))

        term = [
            wide(weight_ref, r) * wide(state_ref, r) * jnp.exp(-wide(decay_ref, r) * ahead)
            for r in range(modes)
        ]
        lam = [jnp.exp(-float(SUBS) * wide(decay_ref, r)) for r in range(modes)]
        for first in range(0, base_ref.shape[0], SUBS):
            parts = list(term)
            while len(parts) > 1:
                parts = [a + b for a, b in zip(parts[::2], parts[1::2])]
            out_ref[first : first + SUBS, lanes] = base_ref[first : first + SUBS, lanes] + parts[0]
            term = [t * l for t, l in zip(term, lam)]
        return carry

    lax.fori_loop(0, tiles, tile, 0)


def split_masks(params_ref, lanes, modes, cached):
    return float(cached) - jnp.broadcast_to(params_ref[modes : modes + 1, lanes], (SUBS, LANES))


def select_kernel(modes, cached, place_ref, slots_ref, pool_ref, *rest):
    param_refs, parcel_ref = rest[:-1], rest[-1]
    groups = len(param_refs)
    pencils = param_refs[0].shape[1] // LANES
    blocks = slots_ref.shape[0] // RANKS
    span = float(cached // blocks)
    slots = [slots_ref[i] for i in range(blocks * RANKS)]
    for hop, params_ref in enumerate(param_refs):
        group = lax.rem(place_ref[0] + (groups - hop), groups)

        def pencil(index, carry, params_ref=params_ref, group=group):
            lanes = pl.ds(pl.multiple_of(index * LANES, LANES), LANES)
            dest = group * pencils + index
            far = pl.ds(pl.multiple_of(dest * LANES, LANES), LANES)
            first = split_masks(params_ref, lanes, modes, cached)

            def page(block, rank):
                return pool_ref[slots[block * RANKS + rank], :, far].astype(jnp.float32)

            for kind in range(KEPT):
                for rank in range(RANKS):
                    value = page(kind, rank)
                    for block in range(kind + KEPT, blocks, KEPT):
                        later = first >= span * float(block - KEPT + 1)
                        value = jnp.where(later, page(block, rank), value)
                    parcel_ref[dest, kind * RANKS + rank] = value.astype(jnp.bfloat16)
            return carry

        lax.fori_loop(0, pencils, pencil, 0, unroll=2)


def state_kernel(modes, cached, place_ref, count_ref, slots_ref, where_ref, pool_ref, *rest):
    param_refs, (_, state_ref, powers) = rest[:-3], rest[-3:]
    groups = len(param_refs)
    pencils = param_refs[0].shape[1] // LANES
    last_page = cached // SUBS - 1
    rows = lax.broadcasted_iota(jnp.int32, (SUBS, LANES), 0).astype(jnp.float32)
    pairs = (count_ref[0] + 1) // 2
    for hop, params_ref in enumerate(param_refs):
        group = lax.rem(place_ref[0] + (groups - hop), groups)

        def pencil(index, carry, params_ref=params_ref, group=group):
            lanes = pl.ds(pl.multiple_of(index * LANES, LANES), LANES)
            dest = group * pencils + index
            far = pl.ds(pl.multiple_of(dest * LANES, LANES), LANES)
            first = split_masks(params_ref, lanes, modes, cached)
            decay = params_ref[0:modes, lanes]

            def prepare(pair, carry):
                for part in range(2):
                    entry = pair * 2 + part
                    ahead = ((last_page - where_ref[entry]) * SUBS).astype(jnp.float32)
                    powers[entry] = jnp.exp(-decay * ahead)
                return carry

            lax.fori_loop(0, pairs, prepare, 0)

            def gather(pair, states):
                for part in range(2):
                    entry = pair * 2 + part
                    value = pool_ref[slots_ref[entry], :, far].astype(jnp.float32)
                    position = (where_ref[entry] * SUBS).astype(jnp.float32) + rows
                    value = jnp.where(position > first, value, 0.0)
                    states = tuple(
                        s + jnp.broadcast_to(powers[entry, r : r + 1, :], (SUBS, LANES)) * value
                        for r, s in enumerate(states)
                    )
                return states

            zero = jnp.zeros((SUBS, LANES), jnp.float32)
            states = lax.fori_loop(0, pairs, gather, tuple(zero for _ in range(modes)))
            for r in range(modes):
                rate = jnp.broadcast_to(params_ref[r : r + 1, lanes], (SUBS, LANES))
                weighted = states[r] * jnp.exp(-rate * (float(SUBS - 1) - rows))
                state_ref[group, r : r + 1, lanes] = jnp.sum(weighted, axis=0, keepdims=True)
            return carry

        lax.fori_loop(0, pencils, pencil, 0)


def tail_kernel(
    modes, steps, blocks, order_ref, pages_ref, length_ref, decay_ref, weight_ref, out_ref, signal, result
):
    cached = order_ref.shape[0] * SUBS
    per_block = order_ref.shape[0] // blocks
    span = per_block * SUBS
    rows = lax.broadcasted_iota(jnp.int32, (SUBS, LANES), 0)
    length = jnp.broadcast_to(length_ref[...], (SUBS, LANES))
    first = cached - length
    from_block = [first >= span * block for block in range(blocks)]
    turn = []
    for kind in range(KEPT):
        member = None
        for block in range(kind, blocks, KEPT):
            here = from_block[block]
            if block + 1 < blocks:
                here = here & jnp.logical_not(from_block[block + 1])
            member = here if member is None else member | here
        turn.append(member)

    def place(index, carry):
        kinds = []
        for kind in range(KEPT):
            value = pages_ref[order_ref[kind * per_block + index]].astype(jnp.float32)
            for block in range(kind + KEPT, blocks, KEPT):
                other = pages_ref[order_ref[block * per_block + index]].astype(jnp.float32)
                value = jnp.where(from_block[block - KEPT + 1], other, value)
            kinds.append(value)
        start = pl.multiple_of(index * SUBS, SUBS)
        for ahead in range(KEPT):
            value = jnp.where(
                turn[1],
                kinds[(1 + ahead) % KEPT],
                jnp.where(turn[2], kinds[(2 + ahead) % KEPT], kinds[ahead]),
            )
            signal[pl.ds(start + ahead * span, SUBS), :] = value
        return carry

    lax.fori_loop(0, per_block, place, 0, unroll=2)

    window = steps * SUBS
    shift = span // 2
    while shift >= 1:
        count = -(-(window + shift - 1) // CHUNK)
        wide = (jnp.broadcast_to(first[0:1, :], (CHUNK, LANES)) & shift) != 0

        def move(index, carry, wide=wide, shift=shift):
            start = pl.multiple_of(index * CHUNK, CHUNK)
            near = signal[pl.ds(start, CHUNK), :]
            far = signal[pl.ds(start + shift, CHUNK), :]
            signal[pl.ds(start, CHUNK), :] = jnp.where(wide, far, near)
            return carry

        lax.fori_loop(0, count, move, 0)
        shift //= 2
    signal[0:SUBS, :] = jnp.where(rows > 0, signal[0:SUBS, :], 0.0)

    lam = [jnp.exp(-row(decay_ref, r)) for r in range(modes)]

    def read(step):
        return signal[pl.ds(step, SUBS, stride=steps), :]

    def write(step, value):
        result[pl.ds(step, SUBS, stride=steps), :] = value

    ends = segment_states(read, steps, lam)
    length_float = length.astype(jnp.float32)
    gain = [
        -row(weight_ref, r) * jnp.exp(-row(decay_ref, r) * length_float) for r in range(modes)
    ]
    begin = [
        gain[r] * shift_down(inclusive_scan(ends[r], row(decay_ref, r), steps), 1)
        for r in range(modes)
    ]
    segment_outputs(read, write, steps, lam, gain, begin)
    out_ref[...] = result[...].astype(jnp.bfloat16)


def gate_kernel(conv_ref, base_ref, gate_ref, out_ref):
    for block in range(conv_ref.shape[0]):
        lanes = slice(block * LANES, (block + 1) * LANES)
        mixed = conv_ref[block].astype(jnp.float32) + base_ref[:, lanes]
        out_ref[:, lanes] = (gate_ref[:, lanes].astype(jnp.float32) * mixed).astype(jnp.bfloat16)


def vmem(count):
    return [pl.BlockSpec(memory_space=pltpu.VMEM) for _ in range(count)]


def params():
    return pltpu.CompilerParams(vmem_limit_bytes=VMEM_LIMIT)


def window_conv(window, decay, weight, skip):
    rows, width = window.shape
    modes = decay.shape[0]
    return pl.pallas_call(
        functools.partial(window_kernel, modes, rows // SUBS),
        out_shape=(
            jax.ShapeDtypeStruct((rows, width), jnp.float32),
            jax.ShapeDtypeStruct((modes, width), jnp.float32),
        ),
        in_specs=vmem(4),
        out_specs=tuple(vmem(2)),
        scratch_shapes=[pltpu.VMEM((rows, LANES), jnp.float32)] * 2,
        compiler_params=params(),
        cost_estimate=pl.CostEstimate(
            flops=12 * rows * width * modes, bytes_accessed=6 * rows * width, transcendentals=0
        ),
        name="window_conv",
    )(window, decay, weight, skip)


def add_carry(base, state, decay, weight):
    rows, width = base.shape
    modes = decay.shape[0]
    return pl.pallas_call(
        functools.partial(carry_kernel, modes),
        out_shape=jax.ShapeDtypeStruct((rows, width), jnp.float32),
        in_specs=vmem(4),
        out_specs=pl.BlockSpec(memory_space=pltpu.VMEM),
        compiler_params=params(),
        cost_estimate=pl.CostEstimate(
            flops=3 * rows * width * modes, bytes_accessed=8 * rows * width, transcendentals=0
        ),
        name="add_carry",
    )(base, state, decay, weight)


def smem(count):
    return [pl.BlockSpec(memory_space=pltpu.SMEM) for _ in range(count)]


def select_pages(place, slots, pool, params_of, modes, cached):
    groups = len(params_of)
    pencils = params_of[0].shape[1] // LANES
    shape = (groups * pencils, KEPT * RANKS, pool.shape[1], LANES)
    return pl.pallas_call(
        functools.partial(select_kernel, modes, cached),
        out_shape=jax.ShapeDtypeStruct(shape, pool.dtype),
        in_specs=smem(2) + vmem(1 + groups),
        out_specs=pl.BlockSpec(memory_space=pltpu.VMEM),
        compiler_params=params(),
        name="select_pages",
    )(place, slots, pool, *params_of)


def page_states(place, count, slots, where, pool, params_of, parcel, modes, cached):
    groups = len(params_of)
    width = params_of[0].shape[1]
    return pl.pallas_call(
        functools.partial(state_kernel, modes, cached),
        out_shape=jax.ShapeDtypeStruct((groups, modes, width), jnp.float32),
        in_specs=smem(4) + vmem(1 + groups) + [pl.BlockSpec(memory_space=pl.ANY)],
        out_specs=pl.BlockSpec(memory_space=pltpu.VMEM),
        scratch_shapes=[pltpu.VMEM((slots.shape[0], modes, LANES), jnp.float32)],
        compiler_params=params(),
        cost_estimate=pl.CostEstimate(
            flops=4 * pool.size * modes, bytes_accessed=2 * pool.size, transcendentals=0
        ),
        name="page_states",
    )(place, count, slots, where, pool, *params_of, parcel)


def tail_conv(order, pages, length, decay, weight, window, blocks):
    modes = decay.shape[0]
    span = order.shape[0] // blocks * SUBS
    return pl.pallas_call(
        functools.partial(tail_kernel, modes, window // SUBS, blocks),
        out_shape=jax.ShapeDtypeStruct((window, LANES), jnp.bfloat16),
        in_specs=smem(1) + vmem(4),
        out_specs=pl.BlockSpec(memory_space=pltpu.VMEM),
        scratch_shapes=[
            pltpu.VMEM((KEPT * span + CHUNK, LANES), jnp.float32),
            pltpu.VMEM((window, LANES), jnp.float32),
        ],
        compiler_params=params(),
        cost_estimate=pl.CostEstimate(
            flops=12 * window * LANES * modes, bytes_accessed=8 * window * LANES, transcendentals=0
        ),
        name="tail_conv",
    )(order, pages, length, decay, weight)


def gate_out(conv_home, base, gate_values):
    return pl.pallas_call(
        gate_kernel,
        out_shape=jax.ShapeDtypeStruct(gate_values.shape, jnp.bfloat16),
        in_specs=vmem(3),
        out_specs=pl.BlockSpec(memory_space=pltpu.VMEM),
        compiler_params=params(),
        name="gate_out",
    )(conv_home, base, gate_values)


def start_states(ends, decay, rows, count):
    state = lax.ppermute(ends, "ctx", [(i, i + 1) for i in range(count - 1)])
    hop = 1
    while hop < count:
        before = lax.ppermute(state, "ctx", [(i, i + hop) for i in range(count - hop)])
        state = state + jnp.exp(-decay * float(rows * hop)) * before
        hop *= 2
    return state


def spread(value, axis, count):
    return [value] + [
        lax.ppermute(value, axis, [(i, (i + hop) % count) for i in range(count)])
        for hop in range(1, count)
    ]


def sum_halving(value, axis, place, count):
    hop = 1
    while hop < count:
        bit = place // hop % 2
        pairs = value.reshape(value.shape[0] // 2, 2, *value.shape[1:])
        keep = lax.dynamic_index_in_dim(pairs, bit, 1, keepdims=False)
        send = lax.dynamic_index_in_dim(pairs, 1 - bit, 1, keepdims=False)
        value = keep + lax.ppermute(send, axis, [(i, i ^ hop) for i in range(count)])
        hop *= 2
    return value[0]


def sum_doubling(value, axis, count):
    hop = 1
    while hop < count:
        value = value + lax.ppermute(value, axis, [(i, i ^ hop) for i in range(count)])
        hop *= 2
    return value


def local(
    window_input, gate_values, page_pool, page_table, filter_len, residues, decays, skip_gain
):
    ctx_count = lax.axis_size("ctx")
    chan_count = lax.axis_size("chan")
    ctx_pos = lax.axis_index("ctx")
    chan_pos = lax.axis_index("chan")
    pool_pages, page_len, _ = page_pool.shape
    rows, slab = window_input.shape
    modes = decays.shape[1]
    pencil = slab // ctx_count
    cached = page_table.shape[0] * page_len
    rates = decays.T
    weights = residues.T

    packed = jnp.concatenate([rates, filter_len.astype(jnp.float32)[None, :]], axis=0)
    params_of = spread(packed, "chan", chan_count)

    owners = page_table // pool_pages
    slots = page_table % pool_pages
    table = owners.reshape(ctx_count, -1)
    per_block = table.shape[1]
    index = jnp.arange(per_block, dtype=jnp.int32)
    earlier = (table[:, :, None] == table[:, None, :]) & (index[None, :] < index[:, None])[None]
    rank = jnp.sum(earlier.astype(jnp.int32), axis=2)
    block = jnp.arange(ctx_count, dtype=jnp.int32)[:, None]
    source = table % chan_count * ctx_count + table // chan_count
    order = (source * (KEPT * RANKS) + block % KEPT * RANKS + rank).reshape(-1)
    mine = table == ctx_pos * chan_count + chan_pos
    picked = mine[:, None, :] & (rank[:, None, :] == jnp.arange(RANKS, dtype=jnp.int32)[None, :, None])
    slot_rows = slots.reshape(ctx_count, 1, per_block)
    send_slots = jnp.sum(jnp.where(picked, slot_rows, 0), axis=2).reshape(-1)
    page_rows = jnp.arange(page_table.shape[0], dtype=jnp.int32).reshape(ctx_count, 1, per_block)
    send_pages = jnp.sum(jnp.where(picked, page_rows + 1, 0), axis=2).reshape(-1) - 1
    used = send_pages >= 0
    entry = jnp.arange(used.shape[0], dtype=jnp.int32)
    before = jnp.sum((used[None, :] & (entry[None, :] < entry[:, None])).astype(jnp.int32), axis=1)
    chosen = used[None, :] & (before[None, :] == entry[:, None])
    list_slots = jnp.sum(jnp.where(chosen, send_slots[None, :], 0), axis=1)
    list_pages = jnp.sum(jnp.where(chosen, send_pages[None, :] + 1, 0), axis=1) - 1
    count = jnp.sum(used.astype(jnp.int32))

    base, ends = window_conv(window_input, rates, weights, skip_gain[None, :])
    state = start_states(ends, rates, rows, ctx_count)

    parcel = select_pages(chan_pos[None], send_slots, page_pool, params_of, modes, cached)
    arrived = lax.all_to_all(parcel, ("chan", "ctx"), split_axis=0, concat_axis=0, tiled=True)
    arrived = arrived.reshape(-1, page_len, pencil)

    from_pages = page_states(
        chan_pos[None], count[None], list_slots, list_pages, page_pool, params_of, parcel, modes, cached
    )
    from_cache = sum_halving(from_pages, "chan", chan_pos, chan_count)
    from_cache = sum_doubling(from_cache, "ctx", ctx_count)
    state = state + jnp.exp(-rates * (ctx_pos * rows).astype(jnp.float32)) * from_cache
    base = add_carry(base, state, rates, weights)

    start = ctx_pos * pencil
    rate = lax.dynamic_slice_in_dim(rates, start, pencil, 1)
    weight = lax.dynamic_slice_in_dim(weights, start, pencil, 1)
    length = lax.dynamic_slice_in_dim(filter_len, start, pencil, 0)[None, :]
    tail = tail_conv(order, arrived, length, rate, weight, rows * ctx_count, ctx_count)
    tail_home = lax.all_to_all(
        tail.reshape(ctx_count, -1, pencil), "ctx", split_axis=0, concat_axis=0, tiled=True
    )
    return gate_out(tail_home, base, gate_values)


def solution(mesh):
    in_specs = (
        P(("req", "ctx"), "chan"),
        P(("req", "ctx"), "chan"),
        P(("req", "ctx", "chan"), None, None),
        P("req"),
        P("chan"),
        P("chan", None),
        P("chan", None),
        P("chan"),
    )
    out_specs = P(("req", "ctx"), "chan")
    return jax.shard_map(local, mesh=mesh, in_specs=in_specs, out_specs=out_specs, check_vma=False)
```

```python
import functools

import jax
import jax.numpy as jnp
from jax import lax
from jax.experimental import pallas as pl
from jax.experimental.pallas import tpu as pltpu
from jax.sharding import PartitionSpec as P

LANES = 128
SUBS = 8
CHUNK = 128
PIECES = 4
VMEM_LIMIT = 12 * 1024 * 1024
WHOLE_VMEM = 60 * 1024 * 1024


def row(ref, index):
    return jnp.broadcast_to(ref[index : index + 1, :], (SUBS, LANES))


def shift_down(value, count):
    moved = pltpu.roll(value, count, 0)
    rows = lax.broadcasted_iota(jnp.int32, value.shape, 0)
    return jnp.where(rows >= count, moved, 0.0)


def segment_states(read, steps, lam):
    def body(step, states):
        value = read(step)
        return tuple(s * l + value for s, l in zip(states, lam))

    zero = jnp.zeros((SUBS, LANES), jnp.float32)
    return lax.fori_loop(0, steps, body, tuple(zero for _ in lam), unroll=4)


def inclusive_scan(end, decay, steps):
    total = end
    for count in (1, 2, 4):
        total = total + jnp.exp(-decay * float(steps * count)) * shift_down(total, count)
    return total


def segment_outputs(read, write, steps, lam, gain, begin):
    def body(step, states):
        value = read(step)
        new = tuple(s * l + g * value for s, l, g in zip(states, lam, gain))
        parts = list(new)
        while len(parts) > 1:
            parts = [a + b for a, b in zip(parts[::2], parts[1::2])]
        write(step, parts[0])
        return new

    lax.fori_loop(0, steps, body, tuple(begin), unroll=4)


def window_kernel(modes, steps, window_ref, decay_ref, weight_ref, skip_ref, base_ref, end_ref, signal, result):
    tiles = window_ref.shape[1] // LANES

    def tile(index, carry):
        lanes = pl.ds(pl.multiple_of(index * LANES, LANES), LANES)

        def wide(ref, r):
            return jnp.broadcast_to(ref[r : r + 1, lanes], (SUBS, LANES))

        signal[...] = window_ref[:, lanes].astype(jnp.float32)
        lam = [jnp.exp(-wide(decay_ref, r)) for r in range(modes)]
        skip = wide(skip_ref, 0)

        def read(step):
            return signal[pl.ds(step, SUBS, stride=steps), :]

        def write(step, value):
            result[pl.ds(step, SUBS, stride=steps), :] = value + skip * read(step)

        ends = segment_states(read, steps, lam)
        gain = [wide(weight_ref, r) for r in range(modes)]
        begin = []
        for r in range(modes):
            total = inclusive_scan(ends[r], wide(decay_ref, r), steps)
            end_ref[r : r + 1, lanes] = total[SUBS - 1 : SUBS, :]
            begin.append(gain[r] * shift_down(total, 1))
        segment_outputs(read, write, steps, lam, gain, begin)
        base_ref[:, lanes] = result[...]
        return carry

    lax.fori_loop(0, tiles, tile, 0)


def cache_kernel(
    modes, steps, slots_ref, pages_ref, length_ref, decay_ref, weight_ref, tail_ref, begin_ref, signal
):
    page_count = slots_ref.shape[0]
    cached = page_count * SUBS
    rows = lax.broadcasted_iota(jnp.int32, (SUBS, LANES), 0)
    length = jnp.broadcast_to(length_ref[...], (SUBS, LANES))
    first = cached - length

    lam_page = [jnp.exp(-float(SUBS) * row(decay_ref, r)) for r in range(modes)]

    def scan_page(page, states):
        value = pages_ref[slots_ref[page]].astype(jnp.float32)
        start = pl.multiple_of(page * SUBS, SUBS)
        signal[pl.ds(start, SUBS), :] = value
        value = jnp.where(rows + page * SUBS > first, value, 0.0)
        return tuple(s * l + value for s, l in zip(states, lam_page))

    zero = jnp.zeros((SUBS, LANES), jnp.float32)
    states = lax.fori_loop(0, page_count, scan_page, tuple(zero for _ in range(modes)), unroll=16)
    rows_float = rows.astype(jnp.float32)
    for r in range(modes):
        decay = row(decay_ref, r)
        weighted = states[r] * jnp.exp(-decay * (float(SUBS - 1) - rows_float))
        total = jnp.broadcast_to(jnp.sum(weighted, axis=0, keepdims=True), (SUBS, LANES))
        ahead = jnp.exp(-decay * (float(steps) * rows_float))
        begin_ref[r * SUBS : (r + 1) * SUBS, :] = row(weight_ref, r) * total * ahead

    window = steps * SUBS
    shift = cached // 2
    while shift >= 1:
        keep = min(window + shift - 1, cached - shift)
        wide = (jnp.broadcast_to(first[0:1, :], (CHUNK, LANES)) & shift) != 0
        into = tail_ref if shift == 1 else signal

        def move(index, carry, wide=wide, shift=shift, into=into):
            start = pl.multiple_of(index * CHUNK, CHUNK)
            near = signal[pl.ds(start, CHUNK), :]
            far = signal[pl.ds(start + shift, CHUNK), :]
            into[pl.ds(start, CHUNK), :] = jnp.where(wide, far, near)
            return carry

        lax.fori_loop(0, -(-keep // CHUNK), move, 0)
        shift //= 2
    tail_ref[0:SUBS, :] = jnp.where(rows > 0, tail_ref[0:SUBS, :], 0.0)

    def read(step):
        return tail_ref[pl.ds(step, SUBS, stride=steps), :]

    ends = segment_states(read, steps, [jnp.exp(-row(decay_ref, r)) for r in range(modes)])
    length_float = length.astype(jnp.float32)
    for r in range(modes):
        decay = row(decay_ref, r)
        prior = shift_down(inclusive_scan(ends[r], decay, steps), 1)
        gone = row(weight_ref, r) * jnp.exp(-decay * length_float) * prior
        here = slice(r * SUBS, (r + 1) * SUBS)
        begin_ref[here, :] = begin_ref[here, :] - gone


def output_kernel(
    modes, steps, place_ref, length_ref, decay_ref, weight_ref, tail_ref, begin_ref, *rest
):
    end_refs, (out_ref, result, before) = rest[:SUBS], rest[SUBS:]
    for hop, end_ref in enumerate(end_refs):
        segment = lax.rem(place_ref[0] + (SUBS - hop), SUBS)
        before[pl.ds(segment, modes, stride=SUBS), :] = end_ref[...]
    length_float = jnp.broadcast_to(length_ref[...], (SUBS, LANES)).astype(jnp.float32)
    begin, lam, gain = [], [], []
    for r in range(modes):
        decay = row(decay_ref, r)
        here = slice(r * SUBS, (r + 1) * SUBS)
        prior = shift_down(inclusive_scan(before[here, :], decay, steps), 1)
        begin.append(begin_ref[here, :] + row(weight_ref, r) * prior)
        lam.append(jnp.exp(-decay))
        gain.append(-row(weight_ref, r) * jnp.exp(-decay * length_float))

    def read(step):
        return tail_ref[pl.ds(step, SUBS, stride=steps), :]

    def write(step, value):
        result[pl.ds(step, SUBS, stride=steps), :] = value

    segment_outputs(read, write, steps, lam, gain, begin)
    out_ref[...] = result[...].astype(jnp.bfloat16)


def parcel_kernel(pool_ref, parcel_ref):
    pages, page_len, _ = pool_ref.shape
    each = parcel_ref.shape[0] // PIECES

    def piece(from_ref, to_ref):
        for block in range(each):
            to_ref[block] = from_ref[:, :, block * LANES : (block + 1) * LANES]

    pltpu.emit_pipeline(
        piece,
        grid=(PIECES,),
        in_specs=[pl.BlockSpec((pages, page_len, each * LANES), lambda i: (0, 0, i))],
        out_specs=[pl.BlockSpec((each, pages, page_len, LANES), lambda i: (i, 0, 0, 0))],
    )(pool_ref, parcel_ref)


def gate_kernel(conv_ref, base_ref, gate_ref, out_ref):
    for block in range(conv_ref.shape[0]):
        lanes = slice(block * LANES, (block + 1) * LANES)
        mixed = conv_ref[block].astype(jnp.float32) + base_ref[:, lanes]
        out_ref[:, lanes] = (gate_ref[:, lanes].astype(jnp.float32) * mixed).astype(jnp.bfloat16)


def vmem(count):
    return [pl.BlockSpec(memory_space=pltpu.VMEM) for _ in range(count)]


def params(limit=VMEM_LIMIT):
    return pltpu.CompilerParams(vmem_limit_bytes=limit)


def window_conv(window, decay, weight, skip):
    rows, width = window.shape
    modes = decay.shape[0]
    return pl.pallas_call(
        functools.partial(window_kernel, modes, rows // SUBS),
        out_shape=(
            jax.ShapeDtypeStruct((rows, width), jnp.float32),
            jax.ShapeDtypeStruct((modes, width), jnp.float32),
        ),
        in_specs=vmem(4),
        out_specs=tuple(vmem(2)),
        scratch_shapes=[pltpu.VMEM((rows, LANES), jnp.float32)] * 2,
        compiler_params=params(),
        cost_estimate=pl.CostEstimate(
            flops=12 * rows * width * modes, bytes_accessed=6 * rows * width, transcendentals=0
        ),
        name="window_conv",
    )(window, decay, weight, skip)


def cache_conv(slots, pages, length, decay, weight, window):
    modes = decay.shape[0]
    cached = slots.shape[0] * SUBS
    return pl.pallas_call(
        functools.partial(cache_kernel, modes, window // SUBS),
        out_shape=(
            jax.ShapeDtypeStruct((window, LANES), jnp.float32),
            jax.ShapeDtypeStruct((modes * SUBS, LANES), jnp.float32),
        ),
        in_specs=[pl.BlockSpec(memory_space=pltpu.SMEM)] + vmem(4),
        out_specs=tuple(vmem(2)),
        scratch_shapes=[pltpu.VMEM((cached + CHUNK, LANES), jnp.float32)],
        compiler_params=params(),
        cost_estimate=pl.CostEstimate(
            flops=40 * cached * LANES * modes, bytes_accessed=4 * cached * LANES, transcendentals=0
        ),
        name="cache_conv",
    )(slots, pages, length, decay, weight)


def output_conv(place, length, decay, weight, tail, begin, ends):
    modes = decay.shape[0]
    window = tail.shape[0]
    return pl.pallas_call(
        functools.partial(output_kernel, modes, window // SUBS),
        out_shape=jax.ShapeDtypeStruct((window, LANES), jnp.bfloat16),
        in_specs=[pl.BlockSpec(memory_space=pltpu.SMEM)] + vmem(5 + len(ends)),
        out_specs=pl.BlockSpec(memory_space=pltpu.VMEM),
        scratch_shapes=[
            pltpu.VMEM((window, LANES), jnp.float32),
            pltpu.VMEM((modes * SUBS, LANES), jnp.float32),
        ],
        compiler_params=params(),
        name="output_conv",
    )(place, length, decay, weight, tail, begin, *ends)


def parcel_of(pool):
    pages, page_len, width = pool.shape
    return pl.pallas_call(
        parcel_kernel,
        out_shape=jax.ShapeDtypeStruct((width // LANES, pages, page_len, LANES), pool.dtype),
        in_specs=[pl.BlockSpec(memory_space=pl.ANY)],
        out_specs=pl.BlockSpec(memory_space=pl.ANY),
        compiler_params=params(WHOLE_VMEM),
        name="parcel_of",
    )(pool)


def gate_out(conv_home, base, gate_values):
    return pl.pallas_call(
        gate_kernel,
        out_shape=jax.ShapeDtypeStruct(gate_values.shape, jnp.bfloat16),
        in_specs=vmem(3),
        out_specs=pl.BlockSpec(memory_space=pltpu.VMEM),
        compiler_params=params(),
        name="gate_out",
    )(conv_home, base, gate_values)


def end_states(ends, place, count):
    pencil = ends.shape[1] // count

    def block(hop):
        return lax.dynamic_slice_in_dim(ends, (place + hop) % count * pencil, pencil, 1)

    return [block(0)] + [
        lax.ppermute(block(hop), "ctx", [(i, (i + hop) % count) for i in range(count)])
        for hop in range(1, count)
    ]


def local(
    window_input, gate_values, page_pool, page_table, filter_len, residues, decays, skip_gain
):
    ctx_count = lax.axis_size("ctx")
    chan_count = lax.axis_size("chan")
    ctx_pos = lax.axis_index("ctx")
    pool_pages, page_len, width = page_pool.shape
    rows = window_input.shape[0]
    pencil = window_input.shape[1] // ctx_count
    arrived = lax.all_to_all(
        parcel_of(page_pool), ("chan", "ctx"), split_axis=0, concat_axis=0, tiled=True
    )
    arrived = arrived.reshape(-1, page_len, pencil)
    owners = page_table // pool_pages
    source = (owners % chan_count) * ctx_count + owners // chan_count
    slots = source * pool_pages + page_table % pool_pages
    start = ctx_pos * pencil
    decay = lax.dynamic_slice_in_dim(decays, start, pencil, 0).T
    weight = lax.dynamic_slice_in_dim(residues, start, pencil, 0).T
    length = lax.dynamic_slice_in_dim(filter_len, start, pencil, 0)[None, :]
    base, ends = window_conv(window_input, decays.T, residues.T, skip_gain[None, :])
    ends = end_states(ends, ctx_pos, ctx_count)
    tail, begin = cache_conv(slots, arrived, length, decay, weight, rows * ctx_count)
    convolved = output_conv(ctx_pos[None], length, decay, weight, tail, begin, ends)
    conv_home = lax.all_to_all(
        convolved.reshape(ctx_count, -1, pencil), "ctx", split_axis=0, concat_axis=0, tiled=True
    )
    return gate_out(conv_home, base, gate_values)


def solution(mesh):
    in_specs = (
        P(("req", "ctx"), "chan"),
        P(("req", "ctx"), "chan"),
        P(("req", "ctx", "chan"), None, None),
        P("req"),
        P("chan"),
        P("chan", None),
        P("chan", None),
        P("chan"),
    )
    out_specs = P(("req", "ctx"), "chan")
    return jax.shard_map(local, mesh=mesh, in_specs=in_specs, out_specs=out_specs, check_vma=False)
```

```python
import functools

import jax
import jax.numpy as jnp
from jax import lax
from jax.experimental import pallas as pl
from jax.experimental.pallas import tpu as pltpu
from jax.sharding import PartitionSpec as P

LANES = 128
SUBS = 8
CHUNK = 128
PIECES = 8
VMEM_LIMIT = 12 * 1024 * 1024
WHOLE_VMEM = 60 * 1024 * 1024


def row(ref, index):
    return jnp.broadcast_to(ref[index : index + 1, :], (SUBS, LANES))


def shift_down(value, count):
    moved = pltpu.roll(value, count, 0)
    rows = lax.broadcasted_iota(jnp.int32, value.shape, 0)
    return jnp.where(rows >= count, moved, 0.0)


def segment_states(read, steps, lam):
    def body(step, states):
        value = read(step)
        return tuple(s * l + value for s, l in zip(states, lam))

    zero = jnp.zeros((SUBS, LANES), jnp.float32)
    return lax.fori_loop(0, steps, body, tuple(zero for _ in lam), unroll=4)


def inclusive_scan(end, decay, steps):
    total = end
    for count in (1, 2, 4):
        total = total + jnp.exp(-decay * float(steps * count)) * shift_down(total, count)
    return total


def segment_outputs(read, write, steps, lam, gain, begin):
    def body(step, states):
        value = read(step)
        new = tuple(s * l + g * value for s, l, g in zip(states, lam, gain))
        parts = list(new)
        while len(parts) > 1:
            parts = [a + b for a, b in zip(parts[::2], parts[1::2])]
        write(step, parts[0])
        return new

    lax.fori_loop(0, steps, body, tuple(begin), unroll=4)


def window_kernel(modes, steps, window_ref, decay_ref, weight_ref, skip_ref, base_ref, end_ref, signal, result):
    tiles = window_ref.shape[1] // LANES

    def tile(index, carry):
        lanes = pl.ds(pl.multiple_of(index * LANES, LANES), LANES)

        def wide(ref, r):
            return jnp.broadcast_to(ref[r : r + 1, lanes], (SUBS, LANES))

        signal[...] = window_ref[:, lanes].astype(jnp.float32)
        lam = [jnp.exp(-wide(decay_ref, r)) for r in range(modes)]
        skip = wide(skip_ref, 0)

        def read(step):
            return signal[pl.ds(step, SUBS, stride=steps), :]

        def write(step, value):
            result[pl.ds(step, SUBS, stride=steps), :] = value + skip * read(step)

        ends = segment_states(read, steps, lam)
        gain = [wide(weight_ref, r) for r in range(modes)]
        begin = []
        for r in range(modes):
            total = inclusive_scan(ends[r], wide(decay_ref, r), steps)
            end_ref[r : r + 1, lanes] = total[SUBS - 1 : SUBS, :]
            begin.append(gain[r] * shift_down(total, 1))
        segment_outputs(read, write, steps, lam, gain, begin)
        base_ref[:, lanes] = result[...]
        return carry

    lax.fori_loop(0, tiles, tile, 0)


def cache_kernel(
    modes, steps, slots_ref, pages_ref, length_ref, decay_ref, weight_ref, tail_ref, begin_ref, signal
):
    page_count = slots_ref.shape[0]
    cached = page_count * SUBS
    rows = lax.broadcasted_iota(jnp.int32, (SUBS, LANES), 0)
    length = jnp.broadcast_to(length_ref[...], (SUBS, LANES))
    first = cached - length

    window = steps * SUBS
    lam_page = [jnp.exp(-float(SUBS) * row(decay_ref, r)) for r in range(modes)]

    def take_page(page):
        value = pages_ref[slots_ref[page]].astype(jnp.float32)
        signal[pl.ds(pl.multiple_of(page * SUBS, SUBS), SUBS), :] = value
        return value

    def copy_page(page, carry):
        take_page(page)
        return carry

    def scan_page(page, states):
        value = jnp.where(rows + page * SUBS >= first + window, take_page(page), 0.0)
        return tuple(s * l + value for s, l in zip(states, lam_page))

    lax.fori_loop(0, window // SUBS, copy_page, 0, unroll=16)
    zero = tuple(jnp.zeros((SUBS, LANES), jnp.float32) for _ in range(modes))
    states = lax.fori_loop(window // SUBS, page_count, scan_page, zero, unroll=16)
    rows_float = rows.astype(jnp.float32)
    for r in range(modes):
        decay = row(decay_ref, r)
        weighted = states[r] * jnp.exp(-decay * (float(SUBS - 1) - rows_float))
        total = jnp.broadcast_to(jnp.sum(weighted, axis=0, keepdims=True), (SUBS, LANES))
        begin_ref[r * SUBS : (r + 1) * SUBS, :] = total

    shift = cached // 2
    while shift >= 1:
        keep = min(window + shift - 1, cached - shift)
        wide = (jnp.broadcast_to(first[0:1, :], (CHUNK, LANES)) & shift) != 0
        into = tail_ref if shift == 1 else signal

        def move(index, carry, wide=wide, shift=shift, into=into):
            start = pl.multiple_of(index * CHUNK, CHUNK)
            near = signal[pl.ds(start, CHUNK), :]
            far = signal[pl.ds(start + shift, CHUNK), :]
            into[pl.ds(start, CHUNK), :] = jnp.where(wide, far, near)
            return carry

        lax.fori_loop(0, -(-keep // CHUNK), move, 0)
        shift //= 2
    tail_ref[0:SUBS, :] = jnp.where(rows > 0, tail_ref[0:SUBS, :], 0.0)

    def read(step):
        return tail_ref[pl.ds(step, SUBS, stride=steps), :]

    ends = segment_states(read, steps, [jnp.exp(-row(decay_ref, r)) for r in range(modes)])
    length_float = length.astype(jnp.float32)
    for r in range(modes):
        decay = row(decay_ref, r)
        weight = row(weight_ref, r)
        here = slice(r * SUBS, (r + 1) * SUBS)
        total = inclusive_scan(ends[r], decay, steps)
        near = jnp.broadcast_to(total[SUBS - 1 : SUBS, :], (SUBS, LANES))
        cache = begin_ref[here, :] + jnp.exp(-decay * (length_float - float(window))) * near
        ahead = jnp.exp(-decay * (float(steps) * rows_float))
        gone = jnp.exp(-decay * length_float) * shift_down(total, 1)
        begin_ref[here, :] = weight * (cache * ahead - gone)


def output_kernel(
    modes, steps, place_ref, length_ref, decay_ref, weight_ref, tail_ref, begin_ref, *rest
):
    end_refs, (out_ref, result, before) = rest[:SUBS], rest[SUBS:]
    for hop, end_ref in enumerate(end_refs):
        segment = lax.rem(place_ref[0] + (SUBS - hop), SUBS)
        before[pl.ds(segment, modes, stride=SUBS), :] = end_ref[...]
    length_float = jnp.broadcast_to(length_ref[...], (SUBS, LANES)).astype(jnp.float32)
    begin, lam, gain = [], [], []
    for r in range(modes):
        decay = row(decay_ref, r)
        here = slice(r * SUBS, (r + 1) * SUBS)
        prior = shift_down(inclusive_scan(before[here, :], decay, steps), 1)
        begin.append(begin_ref[here, :] + row(weight_ref, r) * prior)
        lam.append(jnp.exp(-decay))
        gain.append(-row(weight_ref, r) * jnp.exp(-decay * length_float))

    def read(step):
        return tail_ref[pl.ds(step, SUBS, stride=steps), :]

    def write(step, value):
        result[pl.ds(step, SUBS, stride=steps), :] = value

    segment_outputs(read, write, steps, lam, gain, begin)
    out_ref[...] = result[...].astype(jnp.bfloat16)


def parcel_kernel(inner, pool_ref, parcel_ref, held, in_sems, out_sems):
    tiles = parcel_ref.shape[0]
    each = tiles // PIECES
    fetches = [
        pltpu.make_async_copy(
            pool_ref.at[:, :, pl.ds(piece * each * LANES, each * LANES)],
            held.at[:, :, pl.ds(piece * each * LANES, each * LANES)],
            in_sems.at[piece],
        )
        for piece in range(PIECES)
    ]
    for fetch in fetches:
        fetch.start()
    sends = []
    for piece, fetch in enumerate(fetches):
        fetch.wait()
        for block in range(piece * each, (piece + 1) * each):
            send = pltpu.make_async_copy(
                held.at[:, :, pl.ds(block * LANES, LANES)], parcel_ref.at[block % inner * (tiles // inner) + block // inner], out_sems.at[block]
            )
            send.start()
            sends.append(send)
    for send in sends:
        send.wait()


def gate_kernel(conv_ref, base_ref, gate_ref, out_ref):
    for block in range(conv_ref.shape[0]):
        lanes = slice(block * LANES, (block + 1) * LANES)
        mixed = conv_ref[block].astype(jnp.float32) + base_ref[:, lanes]
        out_ref[:, lanes] = (gate_ref[:, lanes].astype(jnp.float32) * mixed).astype(jnp.bfloat16)


def vmem(count):
    return [pl.BlockSpec(memory_space=pltpu.VMEM) for _ in range(count)]


def params(limit=VMEM_LIMIT):
    return pltpu.CompilerParams(vmem_limit_bytes=limit)


def window_conv(window, decay, weight, skip):
    rows, width = window.shape
    modes = decay.shape[0]
    return pl.pallas_call(
        functools.partial(window_kernel, modes, rows // SUBS),
        out_shape=(
            jax.ShapeDtypeStruct((rows, width), jnp.float32),
            jax.ShapeDtypeStruct((modes, width), jnp.float32),
        ),
        in_specs=vmem(4),
        out_specs=tuple(vmem(2)),
        scratch_shapes=[pltpu.VMEM((rows, LANES), jnp.float32)] * 2,
        compiler_params=params(),
        cost_estimate=pl.CostEstimate(
            flops=12 * rows * width * modes, bytes_accessed=6 * rows * width, transcendentals=0
        ),
        name="window_conv",
    )(window, decay, weight, skip)


def cache_conv(slots, pages, length, decay, weight, window):
    modes = decay.shape[0]
    cached = slots.shape[0] * SUBS
    return pl.pallas_call(
        functools.partial(cache_kernel, modes, window // SUBS),
        out_shape=(
            jax.ShapeDtypeStruct((window, LANES), jnp.float32),
            jax.ShapeDtypeStruct((modes * SUBS, LANES), jnp.float32),
        ),
        in_specs=[pl.BlockSpec(memory_space=pltpu.SMEM)] + vmem(4),
        out_specs=tuple(vmem(2)),
        scratch_shapes=[pltpu.VMEM((cached + CHUNK, LANES), jnp.float32)],
        compiler_params=params(),
        cost_estimate=pl.CostEstimate(
            flops=40 * cached * LANES * modes, bytes_accessed=4 * cached * LANES, transcendentals=0
        ),
        name="cache_conv",
    )(slots, pages, length, decay, weight)


def output_conv(place, length, decay, weight, tail, begin, ends):
    modes = decay.shape[0]
    window = tail.shape[0]
    return pl.pallas_call(
        functools.partial(output_kernel, modes, window // SUBS),
        out_shape=jax.ShapeDtypeStruct((window, LANES), jnp.bfloat16),
        in_specs=[pl.BlockSpec(memory_space=pltpu.SMEM)] + vmem(5 + len(ends)),
        out_specs=pl.BlockSpec(memory_space=pltpu.VMEM),
        scratch_shapes=[
            pltpu.VMEM((window, LANES), jnp.float32),
            pltpu.VMEM((modes * SUBS, LANES), jnp.float32),
        ],
        compiler_params=params(),
        name="output_conv",
    )(place, length, decay, weight, tail, begin, *ends)


def parcel_of(pool, inner):
    pages, page_len, width = pool.shape
    return pl.pallas_call(
        functools.partial(parcel_kernel, inner),
        out_shape=jax.ShapeDtypeStruct((width // LANES, pages, page_len, LANES), pool.dtype),
        in_specs=[pl.BlockSpec(memory_space=pl.ANY)],
        out_specs=pl.BlockSpec(memory_space=pl.ANY),
        scratch_shapes=[
            pltpu.VMEM(pool.shape, pool.dtype),
            pltpu.SemaphoreType.DMA((PIECES,)),
            pltpu.SemaphoreType.DMA((width // LANES,)),
        ],
        compiler_params=params(WHOLE_VMEM),
        name="parcel_of",
    )(pool)


def gate_out(conv_home, base, gate_values):
    return pl.pallas_call(
        gate_kernel,
        out_shape=jax.ShapeDtypeStruct(gate_values.shape, jnp.bfloat16),
        in_specs=vmem(3),
        out_specs=pl.BlockSpec(memory_space=pltpu.VMEM),
        compiler_params=params(),
        name="gate_out",
    )(conv_home, base, gate_values)


def end_states(ends, place, count):
    pencil = ends.shape[1] // count

    def block(hop):
        return lax.dynamic_slice_in_dim(ends, (place + hop) % count * pencil, pencil, 1)

    return [block(0)] + [
        lax.ppermute(block(hop), "ctx", [(i, (i + hop) % count) for i in range(count)])
        for hop in range(1, count)
    ]


def local(
    window_input, gate_values, page_pool, page_table, filter_len, residues, decays, skip_gain
):
    ctx_count = lax.axis_size("ctx")
    ctx_pos = lax.axis_index("ctx")
    pool_pages, page_len, width = page_pool.shape
    rows = window_input.shape[0]
    pencil = window_input.shape[1] // ctx_count
    arrived = lax.all_to_all(
        parcel_of(page_pool, ctx_count), ("ctx", "chan"), split_axis=0, concat_axis=0, tiled=True
    )
    arrived = arrived.reshape(-1, page_len, pencil)
    start = ctx_pos * pencil
    decay = lax.dynamic_slice_in_dim(decays, start, pencil, 0).T
    weight = lax.dynamic_slice_in_dim(residues, start, pencil, 0).T
    length = lax.dynamic_slice_in_dim(filter_len, start, pencil, 0)[None, :]
    base, ends = window_conv(window_input, decays.T, residues.T, skip_gain[None, :])
    ends = end_states(ends, ctx_pos, ctx_count)
    tail, begin = cache_conv(page_table, arrived, length, decay, weight, rows * ctx_count)
    convolved = output_conv(ctx_pos[None], length, decay, weight, tail, begin, ends)
    conv_home = lax.all_to_all(
        convolved.reshape(ctx_count, -1, pencil), "ctx", split_axis=0, concat_axis=0, tiled=True
    )
    return gate_out(conv_home, base, gate_values)


def solution(mesh):
    in_specs = (
        P(("req", "ctx"), "chan"),
        P(("req", "ctx"), "chan"),
        P(("req", "ctx", "chan"), None, None),
        P("req"),
        P("chan"),
        P("chan", None),
        P("chan", None),
        P("chan"),
    )
    out_specs = P(("req", "ctx"), "chan")
    return jax.shard_map(local, mesh=mesh, in_specs=in_specs, out_specs=out_specs, check_vma=False)
```

```python
import functools

import jax
import jax.numpy as jnp
from jax import lax
from jax.experimental import pallas as pl
from jax.experimental.pallas import tpu as pltpu
from jax.sharding import PartitionSpec as P

LANES = 128
SUBS = 8
CHUNK = 128
PIECES = 2
COUNTS = (13, 14, 15)
VMEM_LIMIT = 12 * 1024 * 1024
WHOLE_VMEM = 60 * 1024 * 1024


def row(ref, index):
    return jnp.broadcast_to(ref[index : index + 1, :], (SUBS, LANES))


def shift_down(value, count):
    moved = pltpu.roll(value, count, 0)
    rows = lax.broadcasted_iota(jnp.int32, value.shape, 0)
    return jnp.where(rows >= count, moved, 0.0)


def segment_states(read, steps, lam):
    def body(step, states):
        value = read(step)
        return tuple(s * l + value for s, l in zip(states, lam))

    zero = jnp.zeros((SUBS, LANES), jnp.float32)
    return lax.fori_loop(0, steps, body, tuple(zero for _ in lam), unroll=4)


def inclusive_scan(end, decay, steps):
    total = end
    for count in (1, 2, 4):
        total = total + jnp.exp(-decay * float(steps * count)) * shift_down(total, count)
    return total


def segment_outputs(read, write, steps, lam, gain, begin):
    def body(step, states):
        value = read(step)
        new = tuple(s * l + g * value for s, l, g in zip(states, lam, gain))
        parts = list(new)
        while len(parts) > 1:
            parts = [a + b for a, b in zip(parts[::2], parts[1::2])]
        write(step, parts[0])
        return new

    lax.fori_loop(0, steps, body, tuple(begin), unroll=4)


def window_kernel(modes, steps, window_ref, decay_ref, weight_ref, skip_ref, base_ref, end_ref, signal, result):
    tiles = window_ref.shape[1] // LANES

    def tile(index, carry):
        lanes = pl.ds(pl.multiple_of(index * LANES, LANES), LANES)

        def wide(ref, r):
            return jnp.broadcast_to(ref[r : r + 1, lanes], (SUBS, LANES))

        signal[...] = window_ref[:, lanes].astype(jnp.float32)
        lam = [jnp.exp(-wide(decay_ref, r)) for r in range(modes)]
        skip = wide(skip_ref, 0)

        def read(step):
            return signal[pl.ds(step, SUBS, stride=steps), :]

        def write(step, value):
            result[pl.ds(step, SUBS, stride=steps), :] = value + skip * read(step)

        ends = segment_states(read, steps, lam)
        gain = [wide(weight_ref, r) for r in range(modes)]
        begin = []
        for r in range(modes):
            total = inclusive_scan(ends[r], wide(decay_ref, r), steps)
            end_ref[r : r + 1, lanes] = total[SUBS - 1 : SUBS, :]
            begin.append(gain[r] * shift_down(total, 1))
        segment_outputs(read, write, steps, lam, gain, begin)
        base_ref[:, lanes] = result[...]
        return carry

    lax.fori_loop(0, tiles, tile, 0)


def cache_kernel(
    modes, steps, slots_ref, pages_ref, length_ref, decay_ref, weight_ref, tail_ref, begin_ref, signal
):
    page_count = slots_ref.shape[0]
    cached = page_count * SUBS
    rows = lax.broadcasted_iota(jnp.int32, (SUBS, LANES), 0)
    length = jnp.broadcast_to(length_ref[...], (SUBS, LANES))
    first = cached - length

    window = steps * SUBS
    lam_page = [jnp.exp(-float(SUBS) * row(decay_ref, r)) for r in range(modes)]

    def take_page(page):
        value = pages_ref[slots_ref[page]].astype(jnp.float32)
        signal[pl.ds(pl.multiple_of(page * SUBS, SUBS), SUBS), :] = value
        return value

    def copy_page(page, carry):
        take_page(page)
        return carry

    def scan_page(page, states):
        value = jnp.where(rows + page * SUBS >= first + window, take_page(page), 0.0)
        return tuple(s * l + value for s, l in zip(states, lam_page))

    lax.fori_loop(0, window // SUBS, copy_page, 0, unroll=16)
    zero = tuple(jnp.zeros((SUBS, LANES), jnp.float32) for _ in range(modes))
    states = lax.fori_loop(window // SUBS, page_count, scan_page, zero, unroll=16)
    rows_float = rows.astype(jnp.float32)
    for r in range(modes):
        decay = row(decay_ref, r)
        weighted = states[r] * jnp.exp(-decay * (float(SUBS - 1) - rows_float))
        total = jnp.broadcast_to(jnp.sum(weighted, axis=0, keepdims=True), (SUBS, LANES))
        begin_ref[r * SUBS : (r + 1) * SUBS, :] = total

    shift = cached // 2
    while shift >= 1:
        keep = min(window + shift - 1, cached - shift)
        wide = (jnp.broadcast_to(first[0:1, :], (CHUNK, LANES)) & shift) != 0
        into = tail_ref if shift == 1 else signal

        def move(index, carry, wide=wide, shift=shift, into=into):
            start = pl.multiple_of(index * CHUNK, CHUNK)
            near = signal[pl.ds(start, CHUNK), :]
            far = signal[pl.ds(start + shift, CHUNK), :]
            into[pl.ds(start, CHUNK), :] = jnp.where(wide, far, near)
            return carry

        lax.fori_loop(0, -(-keep // CHUNK), move, 0)
        shift //= 2
    tail_ref[0:SUBS, :] = jnp.where(rows > 0, tail_ref[0:SUBS, :], 0.0)

    def read(step):
        return tail_ref[pl.ds(step, SUBS, stride=steps), :]

    ends = segment_states(read, steps, [jnp.exp(-row(decay_ref, r)) for r in range(modes)])
    length_float = length.astype(jnp.float32)
    for r in range(modes):
        decay = row(decay_ref, r)
        weight = row(weight_ref, r)
        here = slice(r * SUBS, (r + 1) * SUBS)
        total = inclusive_scan(ends[r], decay, steps)
        near = jnp.broadcast_to(total[SUBS - 1 : SUBS, :], (SUBS, LANES))
        cache = begin_ref[here, :] + jnp.exp(-decay * (length_float - float(window))) * near
        ahead = jnp.exp(-decay * (float(steps) * rows_float))
        gone = jnp.exp(-decay * length_float) * shift_down(total, 1)
        begin_ref[here, :] = weight * (cache * ahead - gone)


def output_kernel(
    modes, steps, place_ref, length_ref, decay_ref, weight_ref, tail_ref, begin_ref, *rest
):
    end_refs, (out_ref, result, before) = rest[:SUBS], rest[SUBS:]
    for hop, end_ref in enumerate(end_refs):
        segment = lax.rem(place_ref[0] + (SUBS - hop), SUBS)
        before[pl.ds(segment, modes, stride=SUBS), :] = end_ref[...]
    length_float = jnp.broadcast_to(length_ref[...], (SUBS, LANES)).astype(jnp.float32)
    begin, lam, gain = [], [], []
    for r in range(modes):
        decay = row(decay_ref, r)
        here = slice(r * SUBS, (r + 1) * SUBS)
        prior = shift_down(inclusive_scan(before[here, :], decay, steps), 1)
        begin.append(begin_ref[here, :] + row(weight_ref, r) * prior)
        lam.append(jnp.exp(-decay))
        gain.append(-row(weight_ref, r) * jnp.exp(-decay * length_float))

    def read(step):
        return tail_ref[pl.ds(step, SUBS, stride=steps), :]

    def write(step, value):
        result[pl.ds(step, SUBS, stride=steps), :] = value

    segment_outputs(read, write, steps, lam, gain, begin)
    out_ref[...] = result[...].astype(jnp.bfloat16)


def plan_kernel(pool_pages, owner_count, counts, self_ref, table_ref, which_ref, list_ref):
    bits = pool_pages.bit_length() - 1
    table = table_ref[...]
    shape = (owner_count, table.shape[1])
    same = lax.shift_right_logical(table, bits) == lax.broadcasted_iota(jnp.int32, shape, 0)
    most = jnp.max(jnp.sum(jnp.where(same, 1.0, 0.0), axis=1, keepdims=True))
    which = jnp.int32(0)
    for count in counts:
        which = which + jnp.where(most > float(count), 1, 0)
    which_ref[0] = which
    mine = lax.broadcasted_iota(jnp.int32, (pool_pages, table.shape[1]), 0) + self_ref[0] * pool_pages
    used = jnp.sum(jnp.where(table == mine, 1.0, 0.0), axis=1, keepdims=True)
    slot = lax.broadcasted_iota(jnp.int32, (pool_pages, LANES), 0)
    lane = lax.broadcasted_iota(jnp.int32, (pool_pages, LANES), 1)
    across = jnp.sum(jnp.where(slot == lane, used, 0.0), axis=0, keepdims=True)
    rank = jnp.sum(jnp.where(lane < slot, across, 0.0), axis=1, keepdims=True)
    here = (used > 0.5) & (rank == lane.astype(jnp.float32))
    chosen = jnp.sum(jnp.where(here, slot.astype(jnp.float32), 0.0), axis=0, keepdims=True)
    list_ref[...] = chosen.astype(jnp.int32)


def parcel_kernel(inner, list_ref, pool_ref, parcel_ref, held, in_sems, out_sems):
    tiles, count = parcel_ref.shape[:2]
    each = tiles // PIECES
    fetches = []
    for piece in range(PIECES):
        lanes = pl.ds(piece * each * LANES, each * LANES)
        for page in range(count):
            fetches.append(
                pltpu.make_async_copy(
                    pool_ref.at[list_ref[0, page], :, lanes],
                    held.at[page, :, lanes],
                    in_sems.at[piece, page],
                )
            )
            fetches[-1].start()
    sends = []
    for piece in range(PIECES):
        for fetch in fetches[piece * count : (piece + 1) * count]:
            fetch.wait()
        for block in range(piece * each, (piece + 1) * each):
            send = pltpu.make_async_copy(
                held.at[:, :, pl.ds(block * LANES, LANES)],
                parcel_ref.at[block % inner * (tiles // inner) + block // inner],
                out_sems.at[block],
            )
            send.start()
            sends.append(send)
    for send in sends:
        send.wait()


def gate_kernel(conv_ref, base_ref, gate_ref, out_ref):
    for block in range(conv_ref.shape[0]):
        lanes = slice(block * LANES, (block + 1) * LANES)
        mixed = conv_ref[block].astype(jnp.float32) + base_ref[:, lanes]
        out_ref[:, lanes] = (gate_ref[:, lanes].astype(jnp.float32) * mixed).astype(jnp.bfloat16)


def vmem(count):
    return [pl.BlockSpec(memory_space=pltpu.VMEM) for _ in range(count)]


def params(limit=VMEM_LIMIT):
    return pltpu.CompilerParams(vmem_limit_bytes=limit)


def window_conv(window, decay, weight, skip):
    rows, width = window.shape
    modes = decay.shape[0]
    return pl.pallas_call(
        functools.partial(window_kernel, modes, rows // SUBS),
        out_shape=(
            jax.ShapeDtypeStruct((rows, width), jnp.float32),
            jax.ShapeDtypeStruct((modes, width), jnp.float32),
        ),
        in_specs=vmem(4),
        out_specs=tuple(vmem(2)),
        scratch_shapes=[pltpu.VMEM((rows, LANES), jnp.float32)] * 2,
        compiler_params=params(),
        cost_estimate=pl.CostEstimate(
            flops=12 * rows * width * modes, bytes_accessed=6 * rows * width, transcendentals=0
        ),
        name="window_conv",
    )(window, decay, weight, skip)


def cache_conv(slots, pages, length, decay, weight, window):
    modes = decay.shape[0]
    cached = slots.shape[0] * SUBS
    return pl.pallas_call(
        functools.partial(cache_kernel, modes, window // SUBS),
        out_shape=(
            jax.ShapeDtypeStruct((window, LANES), jnp.float32),
            jax.ShapeDtypeStruct((modes * SUBS, LANES), jnp.float32),
        ),
        in_specs=[pl.BlockSpec(memory_space=pltpu.SMEM)] + vmem(4),
        out_specs=tuple(vmem(2)),
        scratch_shapes=[pltpu.VMEM((cached + CHUNK, LANES), jnp.float32)],
        compiler_params=params(),
        cost_estimate=pl.CostEstimate(
            flops=40 * cached * LANES * modes, bytes_accessed=4 * cached * LANES, transcendentals=0
        ),
        name="cache_conv",
    )(slots, pages, length, decay, weight)


def output_conv(place, length, decay, weight, tail, begin, ends):
    modes = decay.shape[0]
    window = tail.shape[0]
    return pl.pallas_call(
        functools.partial(output_kernel, modes, window // SUBS),
        out_shape=jax.ShapeDtypeStruct((window, LANES), jnp.bfloat16),
        in_specs=[pl.BlockSpec(memory_space=pltpu.SMEM)] + vmem(5 + len(ends)),
        out_specs=pl.BlockSpec(memory_space=pltpu.VMEM),
        scratch_shapes=[
            pltpu.VMEM((window, LANES), jnp.float32),
            pltpu.VMEM((modes * SUBS, LANES), jnp.float32),
        ],
        compiler_params=params(),
        name="output_conv",
    )(place, length, decay, weight, tail, begin, *ends)


def plan_of(self_owner, table, pool_pages, owner_count, counts):
    return pl.pallas_call(
        functools.partial(plan_kernel, pool_pages, owner_count, counts),
        out_shape=(
            jax.ShapeDtypeStruct((1,), jnp.int32),
            jax.ShapeDtypeStruct((1, LANES), jnp.int32),
        ),
        in_specs=[pl.BlockSpec(memory_space=pltpu.SMEM)] + vmem(1),
        out_specs=(pl.BlockSpec(memory_space=pltpu.SMEM), pl.BlockSpec(memory_space=pltpu.VMEM)),
        compiler_params=params(),
        name="plan_of",
    )(self_owner, table)


def parcel_of(chosen, pool, inner, count):
    _, page_len, width = pool.shape
    return pl.pallas_call(
        functools.partial(parcel_kernel, inner),
        out_shape=jax.ShapeDtypeStruct((width // LANES, count, page_len, LANES), pool.dtype),
        in_specs=[pl.BlockSpec(memory_space=pltpu.SMEM), pl.BlockSpec(memory_space=pl.ANY)],
        out_specs=pl.BlockSpec(memory_space=pl.ANY),
        scratch_shapes=[
            pltpu.VMEM((count, page_len, width), pool.dtype),
            pltpu.SemaphoreType.DMA((PIECES, count)),
            pltpu.SemaphoreType.DMA((width // LANES,)),
        ],
        compiler_params=params(WHOLE_VMEM),
        name="parcel_of",
    )(chosen, pool)


def gate_out(conv_home, base, gate_values):
    return pl.pallas_call(
        gate_kernel,
        out_shape=jax.ShapeDtypeStruct(gate_values.shape, jnp.bfloat16),
        in_specs=vmem(3),
        out_specs=pl.BlockSpec(memory_space=pltpu.VMEM),
        compiler_params=params(),
        name="gate_out",
    )(conv_home, base, gate_values)


def end_states(ends, place, count):
    pencil = ends.shape[1] // count

    def block(hop):
        return lax.dynamic_slice_in_dim(ends, (place + hop) % count * pencil, pencil, 1)

    return [block(0)] + [
        lax.ppermute(block(hop), "ctx", [(i, (i + hop) % count) for i in range(count)])
        for hop in range(1, count)
    ]


def with_count(
    count, window_input, gate_values, page_pool, page_table, chosen, filter_len, residues, decays, skip_gain
):
    ctx_count = lax.axis_size("ctx")
    ctx_pos = lax.axis_index("ctx")
    page_len = page_pool.shape[1]
    rows = window_input.shape[0]
    pencil = window_input.shape[1] // ctx_count
    parcel = parcel_of(chosen, page_pool, ctx_count, count)
    arrived = lax.all_to_all(parcel, ("ctx", "chan"), split_axis=0, concat_axis=0, tiled=True)
    arrived = arrived.reshape(-1, page_len, pencil)
    owners = page_table // page_pool.shape[0]
    lower = (owners[:, None] == owners[None, :]) & (page_table[None, :] < page_table[:, None])
    slots = owners * count + jnp.sum(lower.astype(jnp.int32), axis=1)
    start = ctx_pos * pencil
    decay = lax.dynamic_slice_in_dim(decays, start, pencil, 0).T
    weight = lax.dynamic_slice_in_dim(residues, start, pencil, 0).T
    length = lax.dynamic_slice_in_dim(filter_len, start, pencil, 0)[None, :]
    base, ends = window_conv(window_input, decays.T, residues.T, skip_gain[None, :])
    ends = end_states(ends, ctx_pos, ctx_count)
    tail, begin = cache_conv(slots, arrived, length, decay, weight, rows * ctx_count)
    convolved = output_conv(ctx_pos[None], length, decay, weight, tail, begin, ends)
    conv_home = lax.all_to_all(
        convolved.reshape(ctx_count, -1, pencil), "ctx", split_axis=0, concat_axis=0, tiled=True
    )
    return gate_out(conv_home, base, gate_values)


def local(
    window_input, gate_values, page_pool, page_table, filter_len, residues, decays, skip_gain
):
    chan_count = lax.axis_size("chan")
    pool_pages = page_pool.shape[0]
    self_owner = lax.axis_index("ctx") * chan_count + lax.axis_index("chan")
    owner_count = lax.axis_size("ctx") * chan_count
    counts = [c for c in COUNTS if c < pool_pages]
    which, chosen = plan_of(
        self_owner[None], page_table[None, :], pool_pages, owner_count, counts
    )
    counts.append(pool_pages)
    return lax.switch(
        which[0],
        [functools.partial(with_count, c) for c in counts],
        window_input,
        gate_values,
        page_pool,
        page_table,
        chosen,
        filter_len,
        residues,
        decays,
        skip_gain,
    )


def solution(mesh):
    in_specs = (
        P(("req", "ctx"), "chan"),
        P(("req", "ctx"), "chan"),
        P(("req", "ctx", "chan"), None, None),
        P("req"),
        P("chan"),
        P("chan", None),
        P("chan", None),
        P("chan"),
    )
    out_specs = P(("req", "ctx"), "chan")
    return jax.shard_map(local, mesh=mesh, in_specs=in_specs, out_specs=out_specs, check_vma=False)
```

```python
import functools

import jax
import jax.numpy as jnp
from jax import lax
from jax.experimental import pallas as pl
from jax.experimental.pallas import tpu as pltpu
from jax.sharding import PartitionSpec as P

LANES = 128
SUBS = 8
CHUNK = 128
PIECES = 4
COUNTS = (13, 14, 15)
VMEM_LIMIT = 12 * 1024 * 1024
PLAN_VMEM = 57 * 1024 * 1024
PARCEL_VMEM = 56 * 1024 * 1024


def row(ref, index):
    return jnp.broadcast_to(ref[index : index + 1, :], (SUBS, LANES))


def shift_down(value, count):
    moved = pltpu.roll(value, count, 0)
    rows = lax.broadcasted_iota(jnp.int32, value.shape, 0)
    return jnp.where(rows >= count, moved, 0.0)


def segment_states(read, steps, lam):
    def body(step, states):
        value = read(step)
        return tuple(s * l + value for s, l in zip(states, lam))

    zero = jnp.zeros((SUBS, LANES), jnp.float32)
    return lax.fori_loop(0, steps, body, tuple(zero for _ in lam), unroll=4)


def inclusive_scan(end, decay, steps):
    total = end
    for count in (1, 2, 4):
        total = total + jnp.exp(-decay * float(steps * count)) * shift_down(total, count)
    return total


def segment_outputs(read, write, steps, lam, gain, begin):
    def body(step, states):
        value = read(step)
        new = tuple(s * l + g * value for s, l, g in zip(states, lam, gain))
        parts = list(new)
        while len(parts) > 1:
            parts = [a + b for a, b in zip(parts[::2], parts[1::2])]
        write(step, parts[0])
        return new

    lax.fori_loop(0, steps, body, tuple(begin), unroll=4)


def window_kernel(modes, steps, window_ref, decay_ref, weight_ref, skip_ref, base_ref, end_ref, signal, result):
    tiles = window_ref.shape[1] // LANES

    def tile(index, carry):
        lanes = pl.ds(pl.multiple_of(index * LANES, LANES), LANES)

        def wide(ref, r):
            return jnp.broadcast_to(ref[r : r + 1, lanes], (SUBS, LANES))

        signal[...] = window_ref[:, lanes].astype(jnp.float32)
        lam = [jnp.exp(-wide(decay_ref, r)) for r in range(modes)]
        skip = wide(skip_ref, 0)

        def read(step):
            return signal[pl.ds(step, SUBS, stride=steps), :]

        def write(step, value):
            result[pl.ds(step, SUBS, stride=steps), :] = value + skip * read(step)

        ends = segment_states(read, steps, lam)
        gain = [wide(weight_ref, r) for r in range(modes)]
        begin = []
        for r in range(modes):
            total = inclusive_scan(ends[r], wide(decay_ref, r), steps)
            end_ref[r : r + 1, lanes] = total[SUBS - 1 : SUBS, :]
            begin.append(gain[r] * shift_down(total, 1))
        segment_outputs(read, write, steps, lam, gain, begin)
        base_ref[:, lanes] = result[...]
        return carry

    lax.fori_loop(0, tiles, tile, 0)


def cache_kernel(
    modes, steps, slots_ref, pages_ref, length_ref, decay_ref, weight_ref, tail_ref, begin_ref, signal
):
    page_count = slots_ref.shape[0]
    cached = page_count * SUBS
    rows = lax.broadcasted_iota(jnp.int32, (SUBS, LANES), 0)
    length = jnp.broadcast_to(length_ref[...], (SUBS, LANES))
    first = cached - length

    window = steps * SUBS
    lam_page = [jnp.exp(-float(SUBS) * row(decay_ref, r)) for r in range(modes)]

    def take_page(page):
        value = pages_ref[slots_ref[page]].astype(jnp.float32)
        signal[pl.ds(pl.multiple_of(page * SUBS, SUBS), SUBS), :] = value
        return value

    def copy_page(page, carry):
        take_page(page)
        return carry

    def scan_page(page, states):
        value = jnp.where(rows + page * SUBS >= first + window, take_page(page), 0.0)
        return tuple(s * l + value for s, l in zip(states, lam_page))

    lax.fori_loop(0, window // SUBS, copy_page, 0, unroll=16)
    zero = tuple(jnp.zeros((SUBS, LANES), jnp.float32) for _ in range(modes))
    states = lax.fori_loop(window // SUBS, page_count, scan_page, zero, unroll=16)
    rows_float = rows.astype(jnp.float32)
    for r in range(modes):
        decay = row(decay_ref, r)
        weighted = states[r] * jnp.exp(-decay * (float(SUBS - 1) - rows_float))
        total = jnp.broadcast_to(jnp.sum(weighted, axis=0, keepdims=True), (SUBS, LANES))
        begin_ref[r * SUBS : (r + 1) * SUBS, :] = total

    shift = cached // 2
    while shift >= 1:
        keep = min(window + shift - 1, cached - shift)
        wide = (jnp.broadcast_to(first[0:1, :], (CHUNK, LANES)) & shift) != 0
        into = tail_ref if shift == 1 else signal

        def move(index, carry, wide=wide, shift=shift, into=into):
            start = pl.multiple_of(index * CHUNK, CHUNK)
            near = signal[pl.ds(start, CHUNK), :]
            far = signal[pl.ds(start + shift, CHUNK), :]
            into[pl.ds(start, CHUNK), :] = jnp.where(wide, far, near)
            return carry

        lax.fori_loop(0, -(-keep // CHUNK), move, 0)
        shift //= 2
    tail_ref[0:SUBS, :] = jnp.where(rows > 0, tail_ref[0:SUBS, :], 0.0)

    def read(step):
        return tail_ref[pl.ds(step, SUBS, stride=steps), :]

    ends = segment_states(read, steps, [jnp.exp(-row(decay_ref, r)) for r in range(modes)])
    length_float = length.astype(jnp.float32)
    for r in range(modes):
        decay = row(decay_ref, r)
        weight = row(weight_ref, r)
        here = slice(r * SUBS, (r + 1) * SUBS)
        total = inclusive_scan(ends[r], decay, steps)
        near = jnp.broadcast_to(total[SUBS - 1 : SUBS, :], (SUBS, LANES))
        cache = begin_ref[here, :] + jnp.exp(-decay * (length_float - float(window))) * near
        ahead = jnp.exp(-decay * (float(steps) * rows_float))
        gone = jnp.exp(-decay * length_float) * shift_down(total, 1)
        begin_ref[here, :] = weight * (cache * ahead - gone)


def output_kernel(
    modes, steps, place_ref, length_ref, decay_ref, weight_ref, tail_ref, begin_ref, *rest
):
    end_refs, (out_ref, result, before) = rest[:SUBS], rest[SUBS:]
    for hop, end_ref in enumerate(end_refs):
        segment = lax.rem(place_ref[0] + (SUBS - hop), SUBS)
        before[pl.ds(segment, modes, stride=SUBS), :] = end_ref[...]
    length_float = jnp.broadcast_to(length_ref[...], (SUBS, LANES)).astype(jnp.float32)
    begin, lam, gain = [], [], []
    for r in range(modes):
        decay = row(decay_ref, r)
        here = slice(r * SUBS, (r + 1) * SUBS)
        prior = shift_down(inclusive_scan(before[here, :], decay, steps), 1)
        begin.append(begin_ref[here, :] + row(weight_ref, r) * prior)
        lam.append(jnp.exp(-decay))
        gain.append(-row(weight_ref, r) * jnp.exp(-decay * length_float))

    def read(step):
        return tail_ref[pl.ds(step, SUBS, stride=steps), :]

    def write(step, value):
        result[pl.ds(step, SUBS, stride=steps), :] = value

    segment_outputs(read, write, steps, lam, gain, begin)
    out_ref[...] = result[...].astype(jnp.bfloat16)


def plan_kernel(pool_pages, owner_count, counts, self_ref, table_ref, _, which_ref, list_ref):
    bits = pool_pages.bit_length() - 1
    table = table_ref[...]
    shape = (owner_count, table.shape[1])
    same = lax.shift_right_logical(table, bits) == lax.broadcasted_iota(jnp.int32, shape, 0)
    most = jnp.max(jnp.sum(jnp.where(same, 1.0, 0.0), axis=1, keepdims=True))
    which = jnp.int32(0)
    for count in counts:
        which = which + jnp.where(most > float(count), 1, 0)
    which_ref[0] = which
    mine = lax.broadcasted_iota(jnp.int32, (pool_pages, table.shape[1]), 0) + self_ref[0] * pool_pages
    used = jnp.sum(jnp.where(table == mine, 1.0, 0.0), axis=1, keepdims=True)
    slot = lax.broadcasted_iota(jnp.int32, (pool_pages, LANES), 0)
    lane = lax.broadcasted_iota(jnp.int32, (pool_pages, LANES), 1)
    across = jnp.sum(jnp.where(slot == lane, used, 0.0), axis=0, keepdims=True)
    rank = jnp.sum(jnp.where(lane < slot, across, 0.0), axis=1, keepdims=True)
    here = (used > 0.5) & (rank == lane.astype(jnp.float32))
    chosen = jnp.sum(jnp.where(here, slot.astype(jnp.float32), 0.0), axis=0, keepdims=True)
    list_ref[...] = chosen.astype(jnp.int32)


def parcel_kernel(inner, list_ref, pool_ref, parcel_ref, staged, sems):
    tiles, count = parcel_ref.shape[:2]
    outer = tiles // inner
    each = tiles // PIECES
    pages = [list_ref[0, page] for page in range(count)]
    sends = []
    for piece in range(PIECES):

        def cut(index, carry, piece=piece):
            dest = piece * each + index
            tile = lax.rem(dest, outer) * inner + lax.div(dest, outer)
            lanes = pl.ds(pl.multiple_of(tile * LANES, LANES), LANES)
            for page in range(count):
                staged[dest, page] = pool_ref[pages[page], :, lanes]
            return carry

        lax.fori_loop(0, each, cut, 0, unroll=2)
        part = pl.ds(piece * each, each)
        sends.append(pltpu.make_async_copy(staged.at[part], parcel_ref.at[part], sems.at[piece]))
        sends[-1].start()
    for send in sends:
        send.wait()


def gate_kernel(conv_ref, base_ref, gate_ref, out_ref):
    for block in range(conv_ref.shape[0]):
        lanes = slice(block * LANES, (block + 1) * LANES)
        mixed = conv_ref[block].astype(jnp.float32) + base_ref[:, lanes]
        out_ref[:, lanes] = (gate_ref[:, lanes].astype(jnp.float32) * mixed).astype(jnp.bfloat16)


def vmem(count):
    return [pl.BlockSpec(memory_space=pltpu.VMEM) for _ in range(count)]


def params(limit=VMEM_LIMIT):
    return pltpu.CompilerParams(vmem_limit_bytes=limit)


def window_conv(window, decay, weight, skip):
    rows, width = window.shape
    modes = decay.shape[0]
    return pl.pallas_call(
        functools.partial(window_kernel, modes, rows // SUBS),
        out_shape=(
            jax.ShapeDtypeStruct((rows, width), jnp.float32),
            jax.ShapeDtypeStruct((modes, width), jnp.float32),
        ),
        in_specs=vmem(4),
        out_specs=tuple(vmem(2)),
        scratch_shapes=[pltpu.VMEM((rows, LANES), jnp.float32)] * 2,
        compiler_params=params(),
        cost_estimate=pl.CostEstimate(
            flops=12 * rows * width * modes, bytes_accessed=6 * rows * width, transcendentals=0
        ),
        name="window_conv",
    )(window, decay, weight, skip)


def cache_conv(slots, pages, length, decay, weight, window):
    modes = decay.shape[0]
    cached = slots.shape[0] * SUBS
    return pl.pallas_call(
        functools.partial(cache_kernel, modes, window // SUBS),
        out_shape=(
            jax.ShapeDtypeStruct((window, LANES), jnp.float32),
            jax.ShapeDtypeStruct((modes * SUBS, LANES), jnp.float32),
        ),
        in_specs=[pl.BlockSpec(memory_space=pltpu.SMEM)] + vmem(4),
        out_specs=tuple(vmem(2)),
        scratch_shapes=[pltpu.VMEM((cached + CHUNK, LANES), jnp.float32)],
        compiler_params=params(),
        cost_estimate=pl.CostEstimate(
            flops=40 * cached * LANES * modes, bytes_accessed=4 * cached * LANES, transcendentals=0
        ),
        name="cache_conv",
    )(slots, pages, length, decay, weight)


def output_conv(place, length, decay, weight, tail, begin, ends):
    modes = decay.shape[0]
    window = tail.shape[0]
    return pl.pallas_call(
        functools.partial(output_kernel, modes, window // SUBS),
        out_shape=jax.ShapeDtypeStruct((window, LANES), jnp.bfloat16),
        in_specs=[pl.BlockSpec(memory_space=pltpu.SMEM)] + vmem(5 + len(ends)),
        out_specs=pl.BlockSpec(memory_space=pltpu.VMEM),
        scratch_shapes=[
            pltpu.VMEM((window, LANES), jnp.float32),
            pltpu.VMEM((modes * SUBS, LANES), jnp.float32),
        ],
        compiler_params=params(),
        name="output_conv",
    )(place, length, decay, weight, tail, begin, *ends)


def plan_of(self_owner, table, pool, pool_pages, owner_count, counts):
    return pl.pallas_call(
        functools.partial(plan_kernel, pool_pages, owner_count, counts),
        out_shape=(
            jax.ShapeDtypeStruct((1,), jnp.int32),
            jax.ShapeDtypeStruct((1, LANES), jnp.int32),
        ),
        in_specs=[pl.BlockSpec(memory_space=pltpu.SMEM)] + vmem(1) + [pl.BlockSpec(memory_space=pl.ANY)],
        out_specs=(pl.BlockSpec(memory_space=pltpu.SMEM), pl.BlockSpec(memory_space=pltpu.VMEM)),
        compiler_params=params(),
        name="plan_of",
    )(self_owner, table, pool)


def parcel_of(chosen, pool, inner, count):
    _, page_len, width = pool.shape
    shape = (width // LANES, count, page_len, LANES)
    return pl.pallas_call(
        functools.partial(parcel_kernel, inner),
        out_shape=jax.ShapeDtypeStruct(shape, pool.dtype),
        in_specs=[pl.BlockSpec(memory_space=pltpu.SMEM)] + vmem(1),
        out_specs=pl.BlockSpec(memory_space=pl.ANY),
        scratch_shapes=[pltpu.VMEM(shape, pool.dtype), pltpu.SemaphoreType.DMA((PIECES,))],
        compiler_params=params(PARCEL_VMEM),
        name="parcel_of",
    )(chosen, pool)


def gate_out(conv_home, base, gate_values):
    return pl.pallas_call(
        gate_kernel,
        out_shape=jax.ShapeDtypeStruct(gate_values.shape, jnp.bfloat16),
        in_specs=vmem(3),
        out_specs=pl.BlockSpec(memory_space=pltpu.VMEM),
        compiler_params=params(),
        name="gate_out",
    )(conv_home, base, gate_values)


def end_states(ends, place, count):
    pencil = ends.shape[1] // count

    def block(hop):
        return lax.dynamic_slice_in_dim(ends, (place + hop) % count * pencil, pencil, 1)

    return [block(0)] + [
        lax.ppermute(block(hop), "ctx", [(i, (i + hop) % count) for i in range(count)])
        for hop in range(1, count)
    ]


def with_count(
    count, window_input, gate_values, page_pool, page_table, chosen, filter_len, residues, decays, skip_gain
):
    ctx_count = lax.axis_size("ctx")
    ctx_pos = lax.axis_index("ctx")
    page_len = page_pool.shape[1]
    rows = window_input.shape[0]
    pencil = window_input.shape[1] // ctx_count
    parcel = parcel_of(chosen, page_pool, ctx_count, count)
    arrived = lax.all_to_all(parcel, ("ctx", "chan"), split_axis=0, concat_axis=0, tiled=True)
    arrived = arrived.reshape(-1, page_len, pencil)
    owners = page_table // page_pool.shape[0]
    lower = (owners[:, None] == owners[None, :]) & (page_table[None, :] < page_table[:, None])
    slots = owners * count + jnp.sum(lower.astype(jnp.int32), axis=1)
    start = ctx_pos * pencil
    decay = lax.dynamic_slice_in_dim(decays, start, pencil, 0).T
    weight = lax.dynamic_slice_in_dim(residues, start, pencil, 0).T
    length = lax.dynamic_slice_in_dim(filter_len, start, pencil, 0)[None, :]
    base, ends = window_conv(window_input, decays.T, residues.T, skip_gain[None, :])
    ends = end_states(ends, ctx_pos, ctx_count)
    tail, begin = cache_conv(slots, arrived, length, decay, weight, rows * ctx_count)
    convolved = output_conv(ctx_pos[None], length, decay, weight, tail, begin, ends)
    conv_home = lax.all_to_all(
        convolved.reshape(ctx_count, -1, pencil), "ctx", split_axis=0, concat_axis=0, tiled=True
    )
    return gate_out(conv_home, base, gate_values)


def local(
    window_input, gate_values, page_pool, page_table, filter_len, residues, decays, skip_gain
):
    chan_count = lax.axis_size("chan")
    pool_pages = page_pool.shape[0]
    self_owner = lax.axis_index("ctx") * chan_count + lax.axis_index("chan")
    owner_count = lax.axis_size("ctx") * chan_count
    counts = [c for c in COUNTS if c < pool_pages]
    which, chosen = plan_of(
        self_owner[None], page_table[None, :], page_pool, pool_pages, owner_count, counts
    )
    counts.append(pool_pages)
    return lax.switch(
        which[0],
        [functools.partial(with_count, c) for c in counts],
        window_input,
        gate_values,
        page_pool,
        page_table,
        chosen,
        filter_len,
        residues,
        decays,
        skip_gain,
    )


def solution(mesh):
    in_specs = (
        P(("req", "ctx"), "chan"),
        P(("req", "ctx"), "chan"),
        P(("req", "ctx", "chan"), None, None),
        P("req"),
        P("chan"),
        P("chan", None),
        P("chan", None),
        P("chan"),
    )
    out_specs = P(("req", "ctx"), "chan")
    return jax.shard_map(local, mesh=mesh, in_specs=in_specs, out_specs=out_specs, check_vma=False)
```

```python
import functools

import jax
import jax.numpy as jnp
from jax import lax
from jax.experimental import pallas as pl
from jax.experimental.pallas import tpu as pltpu
from jax.sharding import PartitionSpec as P

LANES = 128
SUBS = 8
CHUNK = 128
PIECES = 8
COUNTS = (13, 14, 15)
VMEM_LIMIT = 12 * 1024 * 1024
PLAN_VMEM = 57 * 1024 * 1024
PARCEL_VMEM = 56 * 1024 * 1024


def row(ref, index):
    return jnp.broadcast_to(ref[index : index + 1, :], (SUBS, LANES))


def shift_down(value, count):
    moved = pltpu.roll(value, count, 0)
    rows = lax.broadcasted_iota(jnp.int32, value.shape, 0)
    return jnp.where(rows >= count, moved, 0.0)


def segment_states(read, steps, lam):
    def body(step, states):
        value = read(step)
        return tuple(s * l + value for s, l in zip(states, lam))

    zero = jnp.zeros((SUBS, LANES), jnp.float32)
    return lax.fori_loop(0, steps, body, tuple(zero for _ in lam), unroll=8)


def inclusive_scan(end, decay, steps):
    total = end
    for count in (1, 2, 4):
        total = total + jnp.exp(-decay * float(steps * count)) * shift_down(total, count)
    return total


def segment_outputs(read, write, steps, lam, gain, begin):
    def body(step, states):
        value = read(step)
        new = tuple(s * l + g * value for s, l, g in zip(states, lam, gain))
        parts = list(new)
        while len(parts) > 1:
            parts = [a + b for a, b in zip(parts[::2], parts[1::2])]
        write(step, parts[0])
        return new

    lax.fori_loop(0, steps, body, tuple(begin), unroll=8)


def window_kernel(modes, steps, window_ref, decay_ref, weight_ref, skip_ref, base_ref, end_ref, signal, result):
    tiles = window_ref.shape[1] // LANES

    def tile(index, carry):
        lanes = pl.ds(pl.multiple_of(index * LANES, LANES), LANES)

        def wide(ref, r):
            return jnp.broadcast_to(ref[r : r + 1, lanes], (SUBS, LANES))

        signal[...] = window_ref[:, lanes].astype(jnp.float32)
        lam = [jnp.exp(-wide(decay_ref, r)) for r in range(modes)]
        skip = wide(skip_ref, 0)

        def read(step):
            return signal[pl.ds(step, SUBS, stride=steps), :]

        def write(step, value):
            result[pl.ds(step, SUBS, stride=steps), :] = value + skip * read(step)

        ends = segment_states(read, steps, lam)
        gain = [wide(weight_ref, r) for r in range(modes)]
        begin = []
        for r in range(modes):
            total = inclusive_scan(ends[r], wide(decay_ref, r), steps)
            end_ref[r : r + 1, lanes] = total[SUBS - 1 : SUBS, :]
            begin.append(gain[r] * shift_down(total, 1))
        segment_outputs(read, write, steps, lam, gain, begin)
        base_ref[:, lanes] = result[...]
        return carry

    lax.fori_loop(0, tiles, tile, 0)


def cache_kernel(
    modes, steps, slots_ref, pages_ref, length_ref, decay_ref, weight_ref, tail_ref, begin_ref, signal
):
    page_count = slots_ref.shape[0]
    cached = page_count * SUBS
    rows = lax.broadcasted_iota(jnp.int32, (SUBS, LANES), 0)
    length = jnp.broadcast_to(length_ref[...], (SUBS, LANES))
    first = cached - length

    window = steps * SUBS
    lam_page = [jnp.exp(-float(SUBS) * row(decay_ref, r)) for r in range(modes)]

    def take_page(page):
        value = pages_ref[slots_ref[page]].astype(jnp.float32)
        signal[pl.ds(pl.multiple_of(page * SUBS, SUBS), SUBS), :] = value
        return value

    def copy_page(page, carry):
        take_page(page)
        return carry

    def scan_page(page, states):
        value = jnp.where(rows + page * SUBS >= first + window, take_page(page), 0.0)
        return tuple(s * l + value for s, l in zip(states, lam_page))

    lax.fori_loop(0, window // SUBS, copy_page, 0, unroll=16)
    zero = tuple(jnp.zeros((SUBS, LANES), jnp.float32) for _ in range(modes))
    states = lax.fori_loop(window // SUBS, page_count, scan_page, zero, unroll=16)
    rows_float = rows.astype(jnp.float32)
    for r in range(modes):
        decay = row(decay_ref, r)
        weighted = states[r] * jnp.exp(-decay * (float(SUBS - 1) - rows_float))
        total = jnp.broadcast_to(jnp.sum(weighted, axis=0, keepdims=True), (SUBS, LANES))
        begin_ref[r * SUBS : (r + 1) * SUBS, :] = total

    shift = cached // 2
    while shift >= 1:
        keep = min(window + shift - 1, cached - shift)
        wide = (jnp.broadcast_to(first[0:1, :], (CHUNK, LANES)) & shift) != 0
        into = tail_ref if shift == 1 else signal

        def move(index, carry, wide=wide, shift=shift, into=into):
            start = pl.multiple_of(index * CHUNK, CHUNK)
            near = signal[pl.ds(start, CHUNK), :]
            far = signal[pl.ds(start + shift, CHUNK), :]
            into[pl.ds(start, CHUNK), :] = jnp.where(wide, far, near)
            return carry

        lax.fori_loop(0, -(-keep // CHUNK), move, 0)
        shift //= 2
    tail_ref[0:SUBS, :] = jnp.where(rows > 0, tail_ref[0:SUBS, :], 0.0)

    def read(step):
        return tail_ref[pl.ds(step, SUBS, stride=steps), :]

    ends = segment_states(read, steps, [jnp.exp(-row(decay_ref, r)) for r in range(modes)])
    length_float = length.astype(jnp.float32)
    for r in range(modes):
        decay = row(decay_ref, r)
        weight = row(weight_ref, r)
        here = slice(r * SUBS, (r + 1) * SUBS)
        total = inclusive_scan(ends[r], decay, steps)
        near = jnp.broadcast_to(total[SUBS - 1 : SUBS, :], (SUBS, LANES))
        cache = begin_ref[here, :] + jnp.exp(-decay * (length_float - float(window))) * near
        ahead = jnp.exp(-decay * (float(steps) * rows_float))
        gone = jnp.exp(-decay * length_float) * shift_down(total, 1)
        begin_ref[here, :] = weight * (cache * ahead - gone)


def output_kernel(
    modes, steps, place_ref, length_ref, decay_ref, weight_ref, tail_ref, begin_ref, *rest
):
    end_refs, (out_ref, result, before) = rest[:SUBS], rest[SUBS:]
    for hop, end_ref in enumerate(end_refs):
        segment = lax.rem(place_ref[0] + (SUBS - hop), SUBS)
        before[pl.ds(segment, modes, stride=SUBS), :] = end_ref[...]
    length_float = jnp.broadcast_to(length_ref[...], (SUBS, LANES)).astype(jnp.float32)
    begin, lam, gain = [], [], []
    for r in range(modes):
        decay = row(decay_ref, r)
        here = slice(r * SUBS, (r + 1) * SUBS)
        prior = shift_down(inclusive_scan(before[here, :], decay, steps), 1)
        begin.append(begin_ref[here, :] + row(weight_ref, r) * prior)
        lam.append(jnp.exp(-decay))
        gain.append(-row(weight_ref, r) * jnp.exp(-decay * length_float))

    def read(step):
        return tail_ref[pl.ds(step, SUBS, stride=steps), :]

    def write(step, value):
        result[pl.ds(step, SUBS, stride=steps), :] = value

    segment_outputs(read, write, steps, lam, gain, begin)
    out_ref[...] = result[...].astype(jnp.bfloat16)


def plan_kernel(pool_pages, owner_count, counts, self_ref, table_ref, _, which_ref, list_ref):
    bits = pool_pages.bit_length() - 1
    table = table_ref[...]
    shape = (owner_count, table.shape[1])
    same = lax.shift_right_logical(table, bits) == lax.broadcasted_iota(jnp.int32, shape, 0)
    most = jnp.max(jnp.sum(jnp.where(same, 1.0, 0.0), axis=1, keepdims=True))
    which = jnp.int32(0)
    for count in counts:
        which = which + jnp.where(most > float(count), 1, 0)
    which_ref[0] = which
    mine = lax.broadcasted_iota(jnp.int32, (pool_pages, table.shape[1]), 0) + self_ref[0] * pool_pages
    used = jnp.sum(jnp.where(table == mine, 1.0, 0.0), axis=1, keepdims=True)
    slot = lax.broadcasted_iota(jnp.int32, (pool_pages, LANES), 0)
    lane = lax.broadcasted_iota(jnp.int32, (pool_pages, LANES), 1)
    across = jnp.sum(jnp.where(slot == lane, used, 0.0), axis=0, keepdims=True)
    rank = jnp.sum(jnp.where(lane < slot, across, 0.0), axis=1, keepdims=True)
    here = (used > 0.5) & (rank == lane.astype(jnp.float32))
    chosen = jnp.sum(jnp.where(here, slot.astype(jnp.float32), 0.0), axis=0, keepdims=True)
    list_ref[...] = chosen.astype(jnp.int32)


def parcel_kernel(inner, list_ref, pool_ref, parcel_ref, staged, sems):
    tiles, count = parcel_ref.shape[:2]
    outer = tiles // inner
    each = tiles // PIECES
    pages = [list_ref[0, page] for page in range(count)]
    sends = []
    for piece in range(PIECES):

        def cut(index, carry, piece=piece):
            dest = piece * each + index
            tile = lax.rem(dest, outer) * inner + lax.div(dest, outer)
            lanes = pl.ds(pl.multiple_of(tile * LANES, LANES), LANES)
            for page in range(count):
                staged[dest, page] = pool_ref[pages[page], :, lanes]
            return carry

        lax.fori_loop(0, each, cut, 0, unroll=4)
        part = pl.ds(piece * each, each)
        sends.append(pltpu.make_async_copy(staged.at[part], parcel_ref.at[part], sems.at[piece]))
        sends[-1].start()
    for send in sends:
        send.wait()


def gate_kernel(conv_ref, base_ref, gate_ref, out_ref):
    for block in range(conv_ref.shape[0]):
        lanes = slice(block * LANES, (block + 1) * LANES)
        mixed = conv_ref[block].astype(jnp.float32) + base_ref[:, lanes]
        out_ref[:, lanes] = (gate_ref[:, lanes].astype(jnp.float32) * mixed).astype(jnp.bfloat16)


def vmem(count):
    return [pl.BlockSpec(memory_space=pltpu.VMEM) for _ in range(count)]


def params(limit=VMEM_LIMIT):
    return pltpu.CompilerParams(vmem_limit_bytes=limit)


def window_conv(window, decay, weight, skip):
    rows, width = window.shape
    modes = decay.shape[0]
    return pl.pallas_call(
        functools.partial(window_kernel, modes, rows // SUBS),
        out_shape=(
            jax.ShapeDtypeStruct((rows, width), jnp.float32),
            jax.ShapeDtypeStruct((modes, width), jnp.float32),
        ),
        in_specs=vmem(4),
        out_specs=tuple(vmem(2)),
        scratch_shapes=[pltpu.VMEM((rows, LANES), jnp.float32)] * 2,
        compiler_params=params(),
        cost_estimate=pl.CostEstimate(
            flops=12 * rows * width * modes, bytes_accessed=6 * rows * width, transcendentals=0
        ),
        name="window_conv",
    )(window, decay, weight, skip)


def cache_conv(slots, pages, length, decay, weight, window):
    modes = decay.shape[0]
    cached = slots.shape[0] * SUBS
    return pl.pallas_call(
        functools.partial(cache_kernel, modes, window // SUBS),
        out_shape=(
            jax.ShapeDtypeStruct((window, LANES), jnp.float32),
            jax.ShapeDtypeStruct((modes * SUBS, LANES), jnp.float32),
        ),
        in_specs=[pl.BlockSpec(memory_space=pltpu.SMEM)] + vmem(4),
        out_specs=tuple(vmem(2)),
        scratch_shapes=[pltpu.VMEM((cached + CHUNK, LANES), jnp.float32)],
        compiler_params=params(),
        cost_estimate=pl.CostEstimate(
            flops=40 * cached * LANES * modes, bytes_accessed=4 * cached * LANES, transcendentals=0
        ),
        name="cache_conv",
    )(slots, pages, length, decay, weight)


def output_conv(place, length, decay, weight, tail, begin, ends):
    modes = decay.shape[0]
    window = tail.shape[0]
    return pl.pallas_call(
        functools.partial(output_kernel, modes, window // SUBS),
        out_shape=jax.ShapeDtypeStruct((window, LANES), jnp.bfloat16),
        in_specs=[pl.BlockSpec(memory_space=pltpu.SMEM)] + vmem(5 + len(ends)),
        out_specs=pl.BlockSpec(memory_space=pltpu.VMEM),
        scratch_shapes=[
            pltpu.VMEM((window, LANES), jnp.float32),
            pltpu.VMEM((modes * SUBS, LANES), jnp.float32),
        ],
        compiler_params=params(),
        name="output_conv",
    )(place, length, decay, weight, tail, begin, *ends)


def plan_of(self_owner, table, pool, pool_pages, owner_count, counts):
    return pl.pallas_call(
        functools.partial(plan_kernel, pool_pages, owner_count, counts),
        out_shape=(
            jax.ShapeDtypeStruct((1,), jnp.int32),
            jax.ShapeDtypeStruct((1, LANES), jnp.int32),
        ),
        in_specs=[pl.BlockSpec(memory_space=pltpu.SMEM)] + vmem(1) + [pl.BlockSpec(memory_space=pl.ANY)],
        out_specs=(pl.BlockSpec(memory_space=pltpu.SMEM), pl.BlockSpec(memory_space=pltpu.VMEM)),
        compiler_params=params(),
        name="plan_of",
    )(self_owner, table, pool)


def parcel_of(chosen, pool, inner, count):
    _, page_len, width = pool.shape
    shape = (width // LANES, count, page_len, LANES)
    return pl.pallas_call(
        functools.partial(parcel_kernel, inner),
        out_shape=jax.ShapeDtypeStruct(shape, pool.dtype),
        in_specs=[pl.BlockSpec(memory_space=pltpu.SMEM)] + vmem(1),
        out_specs=pl.BlockSpec(memory_space=pl.ANY),
        scratch_shapes=[pltpu.VMEM(shape, pool.dtype), pltpu.SemaphoreType.DMA((PIECES,))],
        compiler_params=params(PARCEL_VMEM),
        name="parcel_of",
    )(chosen, pool)


def gate_out(conv_home, base, gate_values):
    return pl.pallas_call(
        gate_kernel,
        out_shape=jax.ShapeDtypeStruct(gate_values.shape, jnp.bfloat16),
        in_specs=vmem(3),
        out_specs=pl.BlockSpec(memory_space=pltpu.VMEM),
        compiler_params=params(),
        name="gate_out",
    )(conv_home, base, gate_values)


def end_states(ends, place, count):
    pencil = ends.shape[1] // count

    def block(hop):
        return lax.dynamic_slice_in_dim(ends, (place + hop) % count * pencil, pencil, 1)

    return [block(0)] + [
        lax.ppermute(block(hop), "ctx", [(i, (i + hop) % count) for i in range(count)])
        for hop in range(1, count)
    ]


def with_count(
    count, window_input, gate_values, page_pool, page_table, chosen, filter_len, residues, decays, skip_gain
):
    ctx_count = lax.axis_size("ctx")
    ctx_pos = lax.axis_index("ctx")
    page_len = page_pool.shape[1]
    rows = window_input.shape[0]
    pencil = window_input.shape[1] // ctx_count
    parcel = parcel_of(chosen, page_pool, ctx_count, count)
    arrived = lax.all_to_all(parcel, ("ctx", "chan"), split_axis=0, concat_axis=0, tiled=True)
    arrived = arrived.reshape(-1, page_len, pencil)
    owners = page_table // page_pool.shape[0]
    lower = (owners[:, None] == owners[None, :]) & (page_table[None, :] < page_table[:, None])
    slots = owners * count + jnp.sum(lower.astype(jnp.int32), axis=1)
    start = ctx_pos * pencil
    decay = lax.dynamic_slice_in_dim(decays, start, pencil, 0).T
    weight = lax.dynamic_slice_in_dim(residues, start, pencil, 0).T
    length = lax.dynamic_slice_in_dim(filter_len, start, pencil, 0)[None, :]
    base, ends = window_conv(window_input, decays.T, residues.T, skip_gain[None, :])
    ends = end_states(ends, ctx_pos, ctx_count)
    tail, begin = cache_conv(slots, arrived, length, decay, weight, rows * ctx_count)
    convolved = output_conv(ctx_pos[None], length, decay, weight, tail, begin, ends)
    conv_home = lax.all_to_all(
        convolved.reshape(ctx_count, -1, pencil), "ctx", split_axis=0, concat_axis=0, tiled=True
    )
    return gate_out(conv_home, base, gate_values)


def local(
    window_input, gate_values, page_pool, page_table, filter_len, residues, decays, skip_gain
):
    chan_count = lax.axis_size("chan")
    pool_pages = page_pool.shape[0]
    self_owner = lax.axis_index("ctx") * chan_count + lax.axis_index("chan")
    owner_count = lax.axis_size("ctx") * chan_count
    counts = [c for c in COUNTS if c < pool_pages]
    which, chosen = plan_of(
        self_owner[None], page_table[None, :], page_pool, pool_pages, owner_count, counts
    )
    counts.append(pool_pages)
    return lax.switch(
        which[0],
        [functools.partial(with_count, c) for c in counts],
        window_input,
        gate_values,
        page_pool,
        page_table,
        chosen,
        filter_len,
        residues,
        decays,
        skip_gain,
    )


def solution(mesh):
    in_specs = (
        P(("req", "ctx"), "chan"),
        P(("req", "ctx"), "chan"),
        P(("req", "ctx", "chan"), None, None),
        P("req"),
        P("chan"),
        P("chan", None),
        P("chan", None),
        P("chan"),
    )
    out_specs = P(("req", "ctx"), "chan")
    return jax.shard_map(local, mesh=mesh, in_specs=in_specs, out_specs=out_specs, check_vma=False)
```

```python
import functools

import jax
import jax.numpy as jnp
from jax import lax
from jax.experimental import pallas as pl
from jax.experimental.pallas import tpu as pltpu
from jax.sharding import PartitionSpec as P

LANES = 128
SUBS = 8
CHUNK = 128
PIECES = 8
COUNTS = (12, 13, 14, 15)
VMEM_LIMIT = 12 * 1024 * 1024
PLAN_VMEM = 57 * 1024 * 1024
PARCEL_VMEM = 56 * 1024 * 1024


def row(ref, index):
    return jnp.broadcast_to(ref[index : index + 1, :], (SUBS, LANES))


def shift_down(value, count):
    moved = pltpu.roll(value, count, 0)
    rows = lax.broadcasted_iota(jnp.int32, value.shape, 0)
    return jnp.where(rows >= count, moved, 0.0)


def segment_states(read, steps, lam):
    def body(step, states):
        value = read(step)
        return tuple(s * l + value for s, l in zip(states, lam))

    zero = jnp.zeros((SUBS, LANES), jnp.float32)
    return lax.fori_loop(0, steps, body, tuple(zero for _ in lam), unroll=8)


def inclusive_scan(end, decay, steps):
    total = end
    for count in (1, 2, 4):
        total = total + jnp.exp(-decay * float(steps * count)) * shift_down(total, count)
    return total


def segment_outputs(read, write, steps, lam, gain, begin):
    def body(step, states):
        value = read(step)
        new = tuple(s * l + g * value for s, l, g in zip(states, lam, gain))
        parts = list(new)
        while len(parts) > 1:
            parts = [a + b for a, b in zip(parts[::2], parts[1::2])]
        write(step, parts[0])
        return new

    lax.fori_loop(0, steps, body, tuple(begin), unroll=8)


def window_kernel(modes, steps, window_ref, decay_ref, weight_ref, skip_ref, base_ref, end_ref, signal, result):
    tiles = window_ref.shape[1] // LANES

    def tile(index, carry):
        lanes = pl.ds(pl.multiple_of(index * LANES, LANES), LANES)

        def wide(ref, r):
            return jnp.broadcast_to(ref[r : r + 1, lanes], (SUBS, LANES))

        signal[...] = window_ref[:, lanes].astype(jnp.float32)
        lam = [jnp.exp(-wide(decay_ref, r)) for r in range(modes)]
        skip = wide(skip_ref, 0)

        def read(step):
            return signal[pl.ds(step, SUBS, stride=steps), :]

        def write(step, value):
            result[pl.ds(step, SUBS, stride=steps), :] = value + skip * read(step)

        ends = segment_states(read, steps, lam)
        gain = [wide(weight_ref, r) for r in range(modes)]
        begin = []
        for r in range(modes):
            total = inclusive_scan(ends[r], wide(decay_ref, r), steps)
            end_ref[r : r + 1, lanes] = total[SUBS - 1 : SUBS, :]
            begin.append(gain[r] * shift_down(total, 1))
        segment_outputs(read, write, steps, lam, gain, begin)
        base_ref[:, lanes] = result[...]
        return carry

    lax.fori_loop(0, tiles, tile, 0)


def cache_kernel(
    modes, steps, slots_ref, pages_ref, length_ref, decay_ref, weight_ref, tail_ref, begin_ref, signal
):
    page_count = slots_ref.shape[0]
    cached = page_count * SUBS
    rows = lax.broadcasted_iota(jnp.int32, (SUBS, LANES), 0)
    length = jnp.broadcast_to(length_ref[...], (SUBS, LANES))
    first = cached - length

    window = steps * SUBS
    lam_page = [jnp.exp(-float(SUBS) * row(decay_ref, r)) for r in range(modes)]

    def take_page(page):
        value = pages_ref[slots_ref[page]].astype(jnp.float32)
        signal[pl.ds(pl.multiple_of(page * SUBS, SUBS), SUBS), :] = value
        return value

    def copy_page(page, carry):
        take_page(page)
        return carry

    def scan_page(page, states):
        value = jnp.where(rows + page * SUBS >= first + window, take_page(page), 0.0)
        return tuple(s * l + value for s, l in zip(states, lam_page))

    lax.fori_loop(0, window // SUBS, copy_page, 0, unroll=16)
    zero = tuple(jnp.zeros((SUBS, LANES), jnp.float32) for _ in range(modes))
    states = lax.fori_loop(window // SUBS, page_count, scan_page, zero, unroll=16)
    rows_float = rows.astype(jnp.float32)
    for r in range(modes):
        decay = row(decay_ref, r)
        weighted = states[r] * jnp.exp(-decay * (float(SUBS - 1) - rows_float))
        total = jnp.broadcast_to(jnp.sum(weighted, axis=0, keepdims=True), (SUBS, LANES))
        begin_ref[r * SUBS : (r + 1) * SUBS, :] = total

    shift = cached // 2
    while shift >= 1:
        keep = min(window + shift - 1, cached - shift)
        wide = (jnp.broadcast_to(first[0:1, :], (CHUNK, LANES)) & shift) != 0
        into = tail_ref if shift == 1 else signal

        def move(index, carry, wide=wide, shift=shift, into=into):
            start = pl.multiple_of(index * CHUNK, CHUNK)
            near = signal[pl.ds(start, CHUNK), :]
            far = signal[pl.ds(start + shift, CHUNK), :]
            into[pl.ds(start, CHUNK), :] = jnp.where(wide, far, near)
            return carry

        lax.fori_loop(0, -(-keep // CHUNK), move, 0)
        shift //= 2
    tail_ref[0:SUBS, :] = jnp.where(rows > 0, tail_ref[0:SUBS, :], 0.0)

    def read(step):
        return tail_ref[pl.ds(step, SUBS, stride=steps), :]

    ends = segment_states(read, steps, [jnp.exp(-row(decay_ref, r)) for r in range(modes)])
    length_float = length.astype(jnp.float32)
    for r in range(modes):
        decay = row(decay_ref, r)
        weight = row(weight_ref, r)
        here = slice(r * SUBS, (r + 1) * SUBS)
        total = inclusive_scan(ends[r], decay, steps)
        near = jnp.broadcast_to(total[SUBS - 1 : SUBS, :], (SUBS, LANES))
        cache = begin_ref[here, :] + jnp.exp(-decay * (length_float - float(window))) * near
        ahead = jnp.exp(-decay * (float(steps) * rows_float))
        gone = jnp.exp(-decay * length_float) * shift_down(total, 1)
        begin_ref[here, :] = weight * (cache * ahead - gone)


def output_kernel(
    modes, steps, place_ref, length_ref, decay_ref, weight_ref, tail_ref, begin_ref, *rest
):
    end_refs, (out_ref, result, before) = rest[:SUBS], rest[SUBS:]
    for hop, end_ref in enumerate(end_refs):
        segment = lax.rem(place_ref[0] + (SUBS - hop), SUBS)
        before[pl.ds(segment, modes, stride=SUBS), :] = end_ref[...]
    length_float = jnp.broadcast_to(length_ref[...], (SUBS, LANES)).astype(jnp.float32)
    begin, lam, gain = [], [], []
    for r in range(modes):
        decay = row(decay_ref, r)
        here = slice(r * SUBS, (r + 1) * SUBS)
        prior = shift_down(inclusive_scan(before[here, :], decay, steps), 1)
        begin.append(begin_ref[here, :] + row(weight_ref, r) * prior)
        lam.append(jnp.exp(-decay))
        gain.append(-row(weight_ref, r) * jnp.exp(-decay * length_float))

    def read(step):
        return tail_ref[pl.ds(step, SUBS, stride=steps), :]

    def write(step, value):
        result[pl.ds(step, SUBS, stride=steps), :] = value

    segment_outputs(read, write, steps, lam, gain, begin)
    out_ref[...] = result[...].astype(jnp.bfloat16)


def plan_kernel(pool_pages, owner_count, counts, self_ref, table_ref, _, which_ref, list_ref):
    bits = pool_pages.bit_length() - 1
    table = table_ref[...]
    shape = (owner_count, table.shape[1])
    same = lax.shift_right_logical(table, bits) == lax.broadcasted_iota(jnp.int32, shape, 0)
    most = jnp.max(jnp.sum(jnp.where(same, 1.0, 0.0), axis=1, keepdims=True))
    which = jnp.int32(0)
    for count in counts:
        which = which + jnp.where(most > float(count), 1, 0)
    which_ref[0] = which
    mine = lax.broadcasted_iota(jnp.int32, (pool_pages, table.shape[1]), 0) + self_ref[0] * pool_pages
    used = jnp.sum(jnp.where(table == mine, 1.0, 0.0), axis=1, keepdims=True)
    slot = lax.broadcasted_iota(jnp.int32, (pool_pages, LANES), 0)
    lane = lax.broadcasted_iota(jnp.int32, (pool_pages, LANES), 1)
    across = jnp.sum(jnp.where(slot == lane, used, 0.0), axis=0, keepdims=True)
    rank = jnp.sum(jnp.where(lane < slot, across, 0.0), axis=1, keepdims=True)
    here = (used > 0.5) & (rank == lane.astype(jnp.float32))
    chosen = jnp.sum(jnp.where(here, slot.astype(jnp.float32), 0.0), axis=0, keepdims=True)
    list_ref[...] = chosen.astype(jnp.int32)


def parcel_kernel(inner, list_ref, pool_ref, parcel_ref, staged, sems):
    tiles, count = parcel_ref.shape[:2]
    outer = tiles // inner
    each = tiles // PIECES
    pages = [list_ref[0, page] for page in range(count)]
    sends = []
    for piece in range(PIECES):

        def cut(index, carry, piece=piece):
            dest = piece * each + index
            tile = lax.rem(dest, outer) * inner + lax.div(dest, outer)
            lanes = pl.ds(pl.multiple_of(tile * LANES, LANES), LANES)
            for page in range(count):
                staged[dest, page] = pool_ref[pages[page], :, lanes]
            return carry

        lax.fori_loop(0, each, cut, 0, unroll=4)
        part = pl.ds(piece * each, each)
        sends.append(pltpu.make_async_copy(staged.at[part], parcel_ref.at[part], sems.at[piece]))
        sends[-1].start()
    for send in sends:
        send.wait()


def gate_kernel(conv_ref, base_ref, gate_ref, out_ref):
    for block in range(conv_ref.shape[0]):
        lanes = slice(block * LANES, (block + 1) * LANES)
        mixed = conv_ref[block].astype(jnp.float32) + base_ref[:, lanes]
        out_ref[:, lanes] = (gate_ref[:, lanes].astype(jnp.float32) * mixed).astype(jnp.bfloat16)


def vmem(count):
    return [pl.BlockSpec(memory_space=pltpu.VMEM) for _ in range(count)]


def params(limit=VMEM_LIMIT):
    return pltpu.CompilerParams(vmem_limit_bytes=limit)


def window_conv(window, decay, weight, skip):
    rows, width = window.shape
    modes = decay.shape[0]
    return pl.pallas_call(
        functools.partial(window_kernel, modes, rows // SUBS),
        out_shape=(
            jax.ShapeDtypeStruct((rows, width), jnp.float32),
            jax.ShapeDtypeStruct((modes, width), jnp.float32),
        ),
        in_specs=vmem(4),
        out_specs=tuple(vmem(2)),
        scratch_shapes=[pltpu.VMEM((rows, LANES), jnp.float32)] * 2,
        compiler_params=params(),
        cost_estimate=pl.CostEstimate(
            flops=12 * rows * width * modes, bytes_accessed=6 * rows * width, transcendentals=0
        ),
        name="window_conv",
    )(window, decay, weight, skip)


def cache_conv(slots, pages, length, decay, weight, window):
    modes = decay.shape[0]
    cached = slots.shape[0] * SUBS
    return pl.pallas_call(
        functools.partial(cache_kernel, modes, window // SUBS),
        out_shape=(
            jax.ShapeDtypeStruct((window, LANES), jnp.float32),
            jax.ShapeDtypeStruct((modes * SUBS, LANES), jnp.float32),
        ),
        in_specs=[pl.BlockSpec(memory_space=pltpu.SMEM)] + vmem(4),
        out_specs=tuple(vmem(2)),
        scratch_shapes=[pltpu.VMEM((cached + CHUNK, LANES), jnp.float32)],
        compiler_params=params(),
        cost_estimate=pl.CostEstimate(
            flops=40 * cached * LANES * modes, bytes_accessed=4 * cached * LANES, transcendentals=0
        ),
        name="cache_conv",
    )(slots, pages, length, decay, weight)


def output_conv(place, length, decay, weight, tail, begin, ends):
    modes = decay.shape[0]
    window = tail.shape[0]
    return pl.pallas_call(
        functools.partial(output_kernel, modes, window // SUBS),
        out_shape=jax.ShapeDtypeStruct((window, LANES), jnp.bfloat16),
        in_specs=[pl.BlockSpec(memory_space=pltpu.SMEM)] + vmem(5 + len(ends)),
        out_specs=pl.BlockSpec(memory_space=pltpu.VMEM),
        scratch_shapes=[
            pltpu.VMEM((window, LANES), jnp.float32),
            pltpu.VMEM((modes * SUBS, LANES), jnp.float32),
        ],
        compiler_params=params(),
        name="output_conv",
    )(place, length, decay, weight, tail, begin, *ends)


def plan_of(self_owner, table, pool, pool_pages, owner_count, counts):
    return pl.pallas_call(
        functools.partial(plan_kernel, pool_pages, owner_count, counts),
        out_shape=(
            jax.ShapeDtypeStruct((1,), jnp.int32),
            jax.ShapeDtypeStruct((1, LANES), jnp.int32),
        ),
        in_specs=[pl.BlockSpec(memory_space=pltpu.SMEM)] + vmem(1) + [pl.BlockSpec(memory_space=pl.ANY)],
        out_specs=(pl.BlockSpec(memory_space=pltpu.SMEM), pl.BlockSpec(memory_space=pltpu.VMEM)),
        compiler_params=params(),
        name="plan_of",
    )(self_owner, table, pool)


def parcel_of(chosen, pool, inner, count):
    _, page_len, width = pool.shape
    shape = (width // LANES, count, page_len, LANES)
    return pl.pallas_call(
        functools.partial(parcel_kernel, inner),
        out_shape=jax.ShapeDtypeStruct(shape, pool.dtype),
        in_specs=[pl.BlockSpec(memory_space=pltpu.SMEM)] + vmem(1),
        out_specs=pl.BlockSpec(memory_space=pl.ANY),
        scratch_shapes=[pltpu.VMEM(shape, pool.dtype), pltpu.SemaphoreType.DMA((PIECES,))],
        compiler_params=params(PARCEL_VMEM),
        name="parcel_of",
    )(chosen, pool)


def gate_out(conv_home, base, gate_values):
    return pl.pallas_call(
        gate_kernel,
        out_shape=jax.ShapeDtypeStruct(gate_values.shape, jnp.bfloat16),
        in_specs=vmem(3),
        out_specs=pl.BlockSpec(memory_space=pltpu.VMEM),
        compiler_params=params(),
        name="gate_out",
    )(conv_home, base, gate_values)


def end_states(ends, place, count):
    pencil = ends.shape[1] // count

    def block(hop):
        return lax.dynamic_slice_in_dim(ends, (place + hop) % count * pencil, pencil, 1)

    return [block(0)] + [
        lax.ppermute(block(hop), "ctx", [(i, (i + hop) % count) for i in range(count)])
        for hop in range(1, count)
    ]


def with_count(
    count, window_input, gate_values, page_pool, page_table, chosen, filter_len, residues, decays, skip_gain
):
    ctx_count = lax.axis_size("ctx")
    ctx_pos = lax.axis_index("ctx")
    page_len = page_pool.shape[1]
    rows = window_input.shape[0]
    pencil = window_input.shape[1] // ctx_count
    parcel = parcel_of(chosen, page_pool, ctx_count, count)
    arrived = lax.all_to_all(parcel, ("ctx", "chan"), split_axis=0, concat_axis=0, tiled=True)
    arrived = arrived.reshape(-1, page_len, pencil)
    owners = page_table // page_pool.shape[0]
    lower = (owners[:, None] == owners[None, :]) & (page_table[None, :] < page_table[:, None])
    slots = owners * count + jnp.sum(lower.astype(jnp.int32), axis=1)
    start = ctx_pos * pencil
    decay = lax.dynamic_slice_in_dim(decays, start, pencil, 0).T
    weight = lax.dynamic_slice_in_dim(residues, start, pencil, 0).T
    length = lax.dynamic_slice_in_dim(filter_len, start, pencil, 0)[None, :]
    base, ends = window_conv(window_input, decays.T, residues.T, skip_gain[None, :])
    ends = end_states(ends, ctx_pos, ctx_count)
    tail, begin = cache_conv(slots, arrived, length, decay, weight, rows * ctx_count)
    convolved = output_conv(ctx_pos[None], length, decay, weight, tail, begin, ends)
    conv_home = lax.all_to_all(
        convolved.reshape(ctx_count, -1, pencil), "ctx", split_axis=0, concat_axis=0, tiled=True
    )
    return gate_out(conv_home, base, gate_values)


def local(
    window_input, gate_values, page_pool, page_table, filter_len, residues, decays, skip_gain
):
    chan_count = lax.axis_size("chan")
    pool_pages = page_pool.shape[0]
    self_owner = lax.axis_index("ctx") * chan_count + lax.axis_index("chan")
    owner_count = lax.axis_size("ctx") * chan_count
    counts = [c for c in COUNTS if c < pool_pages]
    which, chosen = plan_of(
        self_owner[None], page_table[None, :], page_pool, pool_pages, owner_count, counts
    )
    counts.append(pool_pages)
    return lax.switch(
        which[0],
        [functools.partial(with_count, c) for c in counts],
        window_input,
        gate_values,
        page_pool,
        page_table,
        chosen,
        filter_len,
        residues,
        decays,
        skip_gain,
    )


def solution(mesh):
    in_specs = (
        P(("req", "ctx"), "chan"),
        P(("req", "ctx"), "chan"),
        P(("req", "ctx", "chan"), None, None),
        P("req"),
        P("chan"),
        P("chan", None),
        P("chan", None),
        P("chan"),
    )
    out_specs = P(("req", "ctx"), "chan")
    return jax.shard_map(local, mesh=mesh, in_specs=in_specs, out_specs=out_specs, check_vma=False)
```
